32 devices in a mesh: section: 2 (over core), ctx: 4 (over y, x), mp: 4 (over z).
Axes of the slice: x: 2, y: 2, z: 4, core: 2. Of those that a mesh axis runs over, the one named last changes fastest.
Arguments:
- section_input: bfloat16 [2, 2048, 2048], P(None, ('ctx', 'mp')), may hold values from -6 to 6
- cotangent: float32 [2, 2048, 2048], P(None, ('ctx', 'mp')), may hold values from -6 to 6
- pair_owner: int32 [2, 2, 4], replicated, may hold values from 0 to 3, each once within a row
- attn_gain: bfloat16 [2, 2048], P('section'), may hold values from 0.5 to 1.5
- w_query: bfloat16 [2, 2048, 2048], P('section', None, 'mp'), may hold values from -0.125 to 0.125
- w_key: bfloat16 [2, 2048, 1024], P('section', None, 'mp'), may hold values from -0.125 to 0.125
- w_value: bfloat16 [2, 2048, 1024], P('section', None, 'mp'), may hold values from -0.125 to 0.125
- query_gain: bfloat16 [2, 128], P('section'), may hold values from 0.099609375 to 1.8984375
- key_gain: bfloat16 [2, 128], P('section'), may hold values from 0.099609375 to 1.8984375
- w_output: bfloat16 [2, 2048, 2048], P('section', 'mp'), may hold values from -0.75 to 0.75
- mlp_gain: bfloat16 [2, 2048], P('section'), may hold values from 0.5 to 1.5
- w_gate: bfloat16 [2, 2048, 6144], P('section', None, 'mp'), may hold values from -0.125 to 0.125
- w_up: bfloat16 [2, 2048, 6144], P('section', None, 'mp'), may hold values from -0.125 to 0.125
- w_down: bfloat16 [2, 6144, 2048], P('section', 'mp'), may hold values from -0.078125 to 0.078125
Outputs:
- section_outputs: float32 [2, 2, 2048, 2048], P('section', None, ('ctx', 'mp'))
- input_grads: float32 [2, 2, 2048, 2048], P('section', None, ('ctx', 'mp'))
- attn_gain_grad: float32 [2, 2048], P('section')
- w_query_grad: float32 [2, 2048, 2048], P('section', None, 'mp')
- w_key_grad: float32 [2, 2048, 1024], P('section', None, 'mp')
- w_value_grad: float32 [2, 2048, 1024], P('section', None, 'mp')
- query_gain_grad: float32 [2, 128], P('section')
- key_gain_grad: float32 [2, 128], P('section')
- w_output_grad: float32 [2, 2048, 2048], P('section', 'mp')
- mlp_gain_grad: float32 [2, 2048], P('section')
- w_gate_grad: float32 [2, 2048, 6144], P('section', None, 'mp')
- w_up_grad: float32 [2, 2048, 6144], P('section', None, 'mp')
- w_down_grad: float32 [2, 6144, 2048], P('section', 'mp')
The draws below stay inside these ranges and needn't reach their ends.
Inputs may be any that keep to these rules, and one draw needn't show every extreme that they name: `pair_owner`: for each micro-batch and sequence, every ctx index appears once.
All inputs are finite; a program needn't handle non-finite values.
Results may differ from the reference program's by a relative error of at most 0.04.
Values may be sent and summed in bfloat16 or wider, within the bound.
No kernel may reach another device: no remote copies, remote signals or barrier semaphores. Data moves between devices by JAX's collectives and lax.ppermute only.
A program may use at most 320 MiB of HBM per device.

```python
from functools import partial
import jax
import jax.numpy as jnp
from jax import lax

D = 2048
QH = 16
KVH = 8
HD = 128
FF = 6144
MB = 2
SEQS = 2
STRETCH = 128
LEN = 1024
TOKENS = 2048
N_CTX = 4


def block_scale(key, extent, pieces, low, high):
    def one(axis_at, parts):
        steps = jax.random.uniform(jax.random.fold_in(jax.random.fold_in(key, 6), axis_at), (parts,), jnp.float32, low / len(pieces), high / len(pieces))
        return jnp.repeat(jnp.exp(steps), extent[axis_at] // parts).reshape((-1,) + (1,) * (len(extent) - axis_at - 1))

    loudness = one(*pieces[0])
    for cut in pieces[1:]:
        loudness = loudness * one(*cut)
    return loudness


def scatter_about(stream_key, extent, deviation, limit, shards=(), kind=jnp.bfloat16):
    factor_of = block_scale(stream_key, extent, shards, -0.22, 0.18) if shards else 1.0
    result = jax.random.normal(stream_key, extent, jnp.float32) * deviation * factor_of
    return jnp.minimum(jnp.maximum(result, -limit), limit).astype(kind)


def setup_inputs(seed: int = 0) -> dict:
    seeds = jax.random.split(jax.random.key(seed), 15)
    return {
        "section_input": scatter_about(seeds[0], (MB, TOKENS, D), 1.0, 6.0, ((1, 16),)),
        "cotangent": scatter_about(seeds[1], (MB, TOKENS, D), 1.0, 6.0, ((1, 16),), jnp.float32),
        "pair_owner": jax.vmap(lambda own: jax.random.permutation(own, N_CTX))(jax.random.split(seeds[2], MB * SEQS)).reshape((MB, SEQS, N_CTX)).astype(jnp.int32),
        "attn_gain": jnp.clip(1.0 + 0.1 * jax.random.normal(seeds[3], (2, D), jnp.float32), 0.5, 1.5).astype(jnp.bfloat16),
        "w_query": scatter_about(seeds[4], (2, D, QH * HD), D ** -0.5, 0.125, ((0, 2), (2, 4))),
        "w_key": scatter_about(seeds[5], (2, D, KVH * HD), D ** -0.5, 0.125, ((0, 2), (2, 4))),
        "w_value": scatter_about(seeds[6], (2, D, KVH * HD), D ** -0.5, 0.125, ((0, 2), (2, 4))),
        "query_gain": jnp.clip(1.0 + 0.18 * jax.random.normal(seeds[7], (2, HD), jnp.float32), 0.099609375, 1.8984375).astype(jnp.bfloat16),
        "key_gain": jnp.clip(1.0 + 0.18 * jax.random.normal(seeds[8], (2, HD), jnp.float32), 0.099609375, 1.8984375).astype(jnp.bfloat16),
        "w_output": scatter_about(seeds[9], (2, QH * HD, D), (QH * HD * 32 // LEN) ** -0.5, 0.75, ((0, 2), (1, 4))),
        "mlp_gain": jnp.clip(1.0 + 0.1 * jax.random.normal(seeds[10], (2, D), jnp.float32), 0.5, 1.5).astype(jnp.bfloat16),
        "w_gate": scatter_about(seeds[11], (2, D, FF), D ** -0.5, 0.125, ((0, 2), (2, 4))),
        "w_up": scatter_about(seeds[12], (2, D, FF), D ** -0.5, 0.125, ((0, 2), (2, 4))),
        "w_down": scatter_about(seeds[13], (2, FF, D), FF ** -0.5, 0.078125, ((0, 2), (1, 4))),
    }


EPSILON = 1e-06
ROPE_BASE = 1000000.0
MASKED_SCORE = -1e+30

@jax.custom_vjp
def low(v):
    return lax.optimization_barrier(v.astype(jnp.bfloat16)).astype(jnp.float32)

@jax.custom_vjp
def low_back(v):
    return v

def low_keep(v):
    return (low(v), None)

def low_pass(kept, grad):
    return (grad,)

def back_keep(v):
    return (v, None)

def back_low(kept, grad):
    return (low(grad),)
low.defvjp(low_keep, low_pass)
low_back.defvjp(back_keep, back_low)

def matmul(left_side, right_side):
    return jnp.dot(left_side, right_side, precision=lax.Precision.HIGHEST, preferred_element_type=jnp.float32)

def row_norm(token_rows, gain_vec):
    scaling = lax.rsqrt(lax.optimization_barrier(jnp.mean(token_rows * token_rows, axis=-1, keepdims=True)) + EPSILON)
    return token_rows * scaling * gain_vec

def rotate(head_split, cosine, sine):
    half_width = head_split.shape[-1] // 2
    front_half = head_split[..., :half_width]
    back_half = head_split[..., half_width:]
    return jnp.concatenate([front_half * cosine - back_half * sine, back_half * cosine + front_half * sine], axis=-1)

def head_prep(flat_rows, gain_vec, cosine, sine):
    row_count = flat_rows.shape[0]
    head_split = flat_rows.reshape(row_count, flat_rows.shape[1] // HD, HD)
    normed = row_norm(head_split, gain_vec)
    return rotate(normed, cosine[:, None, :], sine[:, None, :]).reshape(row_count, flat_rows.shape[1])

def rope_tables(positions):
    inv_freq = ROPE_BASE ** (-jnp.arange(0, HD, 2).astype(jnp.float32) / HD)
    angles = positions.astype(jnp.float32)[:, None] * inv_freq[None, :]
    return (jnp.cos(angles), jnp.sin(angles))

def block_positions(stretch_owner, devices, n_ctx):
    matches = devices[:, None] == jnp.arange(n_ctx, dtype=jnp.int32)[None, :]
    held_block = lax.optimization_barrier(jnp.sum(jnp.where(matches[:, None, :], stretch_owner[None, :, :], 0), axis=-1)).astype(jnp.int32)
    offsets = jnp.arange(STRETCH, dtype=jnp.int32)
    lower_pos = held_block[:, :, None] * STRETCH + offsets[None, None, :]
    upper_pos = (2 * n_ctx - 1 - held_block)[:, :, None] * STRETCH + offsets[None, None, :]
    return jnp.concatenate([lower_pos, upper_pos], axis=-1).astype(jnp.int32)

def one_head(query_rows, key_rows, value_rows, places):
    scores = low_back(matmul(query_rows, key_rows.T) * HD ** (-0.5))
    allowed = places[None, :] <= places[:, None]
    probs = jax.nn.softmax(jnp.where(allowed, scores, MASKED_SCORE), axis=-1)
    return matmul(low(probs), value_rows)

def head_item(item_set):
    return jax.checkpoint(one_head)(item_set[0], item_set[1], item_set[2], item_set[3])

def per_sequence(flat_rows, head_count):
    block_span = 2 * STRETCH
    shaped = flat_rows.reshape(N_CTX, SEQS, block_span, head_count, HD)
    return shaped.transpose(1, 3, 0, 2, 4).reshape(SEQS * head_count, N_CTX * block_span, HD)

def section_layer(stretch_owner, token_rows, attn_gain, w_query, w_key, w_value, query_gain, key_gain, w_output, mlp_gain, w_gate, w_up, w_down):
    block_span = 2 * STRETCH
    seq_length = N_CTX * block_span
    groups = QH // KVH
    places = block_positions(stretch_owner, jnp.arange(N_CTX, dtype=jnp.int32), N_CTX)
    cosine, sine = rope_tables(places.reshape(-1))
    attn_in = low(row_norm(token_rows, attn_gain))
    q_proj = low_back(matmul(attn_in, w_query))
    k_proj = low_back(matmul(attn_in, w_key))
    values = low(low_back(matmul(attn_in, w_value)))
    queries = low(head_prep(q_proj, query_gain, cosine, sine))
    key_rows = low(head_prep(k_proj, key_gain, cosine, sine))
    seq_keys = jnp.repeat(per_sequence(key_rows, KVH).reshape(SEQS, KVH, seq_length, HD), groups, axis=1)
    seq_values = jnp.repeat(per_sequence(values, KVH).reshape(SEQS, KVH, seq_length, HD), groups, axis=1)
    seq_places = jnp.repeat(places.transpose(1, 0, 2).reshape(SEQS, seq_length), QH, axis=0)
    attended = lax.map(head_item, (per_sequence(queries, QH), seq_keys.reshape(SEQS * QH, seq_length, HD), seq_values.reshape(SEQS * QH, seq_length, HD), seq_places))
    attended = attended.reshape(SEQS, QH, N_CTX, block_span, HD).transpose(2, 0, 3, 1, 4).reshape(N_CTX * SEQS * block_span, QH * HD)
    attended_low = low(low_back(attended))
    mid_rows = token_rows + low_back(matmul(attended_low, w_output))
    mlp_in = low(row_norm(mid_rows, mlp_gain))
    gate_pre = low_back(matmul(mlp_in, w_gate))
    up_pre = low_back(matmul(mlp_in, w_up))
    hidden = low(jax.nn.silu(gate_pre) * up_pre)
    return mid_rows + low_back(matmul(hidden, w_down))

def reference(section_input, cotangent, pair_owner, attn_gain, w_query, w_key, w_value, query_gain, key_gain, w_output, mlp_gain, w_gate, w_up, w_down):
    every_weight = (attn_gain, w_query, w_key, w_value, query_gain, key_gain, w_output, mlp_gain, w_gate, w_up, w_down)
    weights = [tuple((array[section_id].astype(jnp.float32) for array in every_weight)) for section_id in range(2)]
    outputs_first, outputs_second, grads_first, grads_second = ([], [], [], [])
    totals_first = [jnp.zeros_like(array) for array in weights[0]]
    totals_second = [jnp.zeros_like(array) for array in weights[1]]
    for micro_index in range(MB):
        layer_fn = partial(section_layer, pair_owner[micro_index])
        first_out, pull_first = jax.vjp(layer_fn, section_input[micro_index].astype(jnp.float32), *weights[0])
        second_out, pull_second = jax.vjp(layer_fn, first_out, *weights[1])
        back_second = pull_second(cotangent[micro_index])
        back_first = pull_first(back_second[0])
        outputs_first.append(first_out)
        outputs_second.append(second_out)
        grads_first.append(back_first[0])
        grads_second.append(back_second[0])
        totals_first = [total_now + grad_now for total_now, grad_now in zip(totals_first, back_first[1:])]
        totals_second = [total_now + grad_now for total_now, grad_now in zip(totals_second, back_second[1:])]
    section_outputs = jnp.stack([jnp.stack(outputs_first), jnp.stack(outputs_second)])
    input_grads = jnp.stack([jnp.stack(grads_first), jnp.stack(grads_second)])
    stacked = [jnp.stack([totals_first[index], totals_second[index]]) for index in range(11)]
    return (section_outputs, input_grads, stacked[0], stacked[1], stacked[2], stacked[3], stacked[4], stacked[5], stacked[6], stacked[7], stacked[8], stacked[9], stacked[10])
```

```python
import functools

import jax
import jax.numpy as jnp
from jax import lax
from jax.experimental import pallas as pl
from jax.experimental.pallas import tpu as pltpu
from jax.sharding import PartitionSpec as P

HD = 128
MB = 2
SEQS = 2
STRETCH = 128
EPSILON = 1e-06
ROPE_BASE = 1000000.0
MASKED_SCORE = -1e30
SCALING = HD ** (-0.5)
LOW = jnp.bfloat16
F32 = jnp.float32
ROW_TILE = 64
VMEM_BYTES = 50 * 1024 * 1024


def dot_nn(left, right):
    return lax.dot_general(left, right, (((1,), (0,)), ((), ())), preferred_element_type=F32)


def dot_nt(left, right):
    return lax.dot_general(left, right, (((1,), (1,)), ((), ())), preferred_element_type=F32)


def dot_tn(left, right):
    return lax.dot_general(left, right, (((0,), (0,)), ((), ())), preferred_element_type=F32)


def kernel_call(body, out_shape, flops, args):
    moved = sum(a.size * a.dtype.itemsize for a in args)
    moved += sum(o.size * o.dtype.itemsize for o in out_shape)
    return pl.pallas_call(
        body,
        out_shape=out_shape,
        compiler_params=pltpu.CompilerParams(vmem_limit_bytes=VMEM_BYTES),
        cost_estimate=pl.CostEstimate(flops=flops, bytes_accessed=moved, transcendentals=0),
    )(*args)


def qkv_forward_body(x, wq, wk, wv, q_gain, k_gain, cosine, sine, q_proj, k_proj, queries, kv):
    rows = x[...]
    cos_full, sin_signed = cosine[...], sine[...]

    def prepared(head, gain):
        scaling = lax.rsqrt(jnp.mean(head * head, axis=-1, keepdims=True) + EPSILON)
        normed = head * scaling * gain
        return (normed * cos_full + pltpu.roll(normed, HD // 2, 1) * sin_signed).astype(LOW)

    k_width = wk.shape[1]
    all_q = dot_nn(rows, wq[...])
    q_proj[...] = all_q
    for at in range(0, wq.shape[1], HD):
        queries[:, at : at + HD] = prepared(all_q[:, at : at + HD], q_gain[...])
    all_k = dot_nn(rows, wk[...])
    k_proj[...] = all_k
    for at in range(0, k_width, HD):
        kv[:, at : at + HD] = prepared(all_k[:, at : at + HD], k_gain[...])
    kv[:, k_width:] = dot_nn(rows, wv[...]).astype(LOW)


def attend_body(n_ctx, queries, *refs):
    blocks = refs[:n_ctx]
    q_pos, k_pos, w_out, part, attended, log_total = refs[n_ctx:]
    rows = queries.shape[0]
    kv_width = blocks[0].shape[1] // 2
    groups = queries.shape[1] // kv_width
    place = jnp.concatenate([q_pos[...]] * groups, axis=0)
    for kv_head in range(kv_width // HD):
        first = kv_head * groups
        stacked = jnp.concatenate(
            [queries[:, (first + i) * HD : (first + i + 1) * HD] for i in range(groups)], axis=0
        )
        at = kv_head * HD
        scores = []
        for j, block in enumerate(blocks):
            raw = dot_nt(stacked, block[:, at : at + HD]) * SCALING
            scores.append(jnp.where(k_pos[j : j + 1, :] <= place, raw, MASKED_SCORE))
        top = functools.reduce(
            jnp.maximum, [jnp.max(s, axis=1, keepdims=True) for s in scores]
        )
        total, running = 0.0, 0.0
        for s, block in zip(scores, blocks):
            weights = jnp.exp(s - top)
            total = total + jnp.sum(weights, axis=1, keepdims=True)
            running = running + dot_nn(
                weights.astype(LOW), block[:, kv_width + at : kv_width + at + HD]
            )
        result = (running / total).astype(LOW)
        logs = top + jnp.log(total)
        for i in range(groups):
            head = first + i
            attended[:, head * HD : (head + 1) * HD] = result[i * rows : (i + 1) * rows]
            log_total[:, head : head + 1] = logs[i * rows : (i + 1) * rows]
    part[...] = dot_nn(attended[...], w_out[...]).astype(LOW)


def attend_back_body(n_ctx, grad_rows, w_out, queries, *refs):
    blocks = refs[:n_ctx]
    q_pos, k_pos, attended, log_total, grad_q = refs[n_ctx : n_ctx + 5]
    grad_kv = refs[n_ctx + 5 :]
    rows = queries.shape[0]
    kv_width = blocks[0].shape[1] // 2
    groups = queries.shape[1] // kv_width
    grad_all = dot_nt(grad_rows[...], w_out[...]).astype(LOW)
    place = jnp.concatenate([q_pos[...]] * groups, axis=0)
    for kv_head in range(kv_width // HD):
        heads = [kv_head * groups + i for i in range(groups)]
        stacked = jnp.concatenate([queries[:, h * HD : (h + 1) * HD] for h in heads], axis=0)
        grads = jnp.concatenate([grad_all[:, h * HD : (h + 1) * HD] for h in heads], axis=0)
        out_low = jnp.concatenate([attended[:, h * HD : (h + 1) * HD] for h in heads], axis=0)
        logs = jnp.concatenate([log_total[:, h : h + 1] for h in heads], axis=0)
        delta = jnp.sum(grads.astype(F32) * out_low.astype(F32), axis=1, keepdims=True)
        at = kv_head * HD
        total = 0.0
        for j, block in enumerate(blocks):
            keys = block[:, at : at + HD]
            values = block[:, kv_width + at : kv_width + at + HD]
            shifted = dot_nt(stacked, keys) * SCALING - logs
            probs = jnp.exp(jnp.where(k_pos[j : j + 1, :] <= place, shifted, MASKED_SCORE))
            grad_scores = (probs * (dot_nt(grads, values) - delta)).astype(LOW)
            total = total + dot_nn(grad_scores, keys)
            grad_kv[j][:, at : at + HD] = (dot_tn(grad_scores, stacked) * SCALING).astype(LOW)
            grad_kv[j][:, kv_width + at : kv_width + at + HD] = dot_tn(
                probs.astype(LOW), grads
            ).astype(LOW)
        for i, h in enumerate(heads):
            grad_q[:, h * HD : (h + 1) * HD] = total[i * rows : (i + 1) * rows] * SCALING


def qkv_back_body(n_ctx, grad_q, *refs):
    grad_kv = refs[:n_ctx]
    q_proj, k_proj, q_gain, k_gain, cosine, sine, wq, wk, wv = refs[n_ctx : n_ctx + 9]
    mixed, part, grad_q_gain, grad_k_gain = refs[n_ctx + 9 :]
    cos_full, sin_signed = cosine[...], sine[...]
    q_width, kv_width = wq.shape[1], wk.shape[1]

    def pulled(grad, head, gain):
        turned = grad * cos_full + pltpu.roll(grad * sin_signed, HD // 2, 1)
        scaling = lax.rsqrt(jnp.mean(head * head, axis=-1, keepdims=True) + EPSILON)
        inner = turned * gain
        back = scaling * inner - head * (
            scaling * scaling * scaling * jnp.mean(inner * head, axis=-1, keepdims=True)
        )
        return back.astype(LOW), jnp.sum(turned * head * scaling, axis=0, keepdims=True)

    total = 0.0
    for at in range(0, q_width, HD):
        back, gain_part = pulled(grad_q[:, at : at + HD], q_proj[:, at : at + HD], q_gain[...])
        mixed[:, at : at + HD] = back
        total = total + gain_part
    grad_q_gain[...] = total
    summed = functools.reduce(jnp.add, [g[...].astype(F32) for g in grad_kv])
    total = 0.0
    for at in range(0, kv_width, HD):
        back, gain_part = pulled(summed[:, at : at + HD], k_proj[:, at : at + HD], k_gain[...])
        mixed[:, q_width + at : q_width + at + HD] = back
        total = total + gain_part
    grad_k_gain[...] = total
    mixed[:, q_width + kv_width :] = summed[:, kv_width:].astype(LOW)
    part[...] = (
        dot_nt(mixed[:, :q_width], wq[...])
        + dot_nt(mixed[:, q_width : q_width + kv_width], wk[...])
        + dot_nt(mixed[:, q_width + kv_width :], wv[...])
    ).astype(LOW)


def assemble_body(pieces, widths, place, *refs):
    ins, outs = refs[: 4 * pieces], refs[4 * pieces :]
    step = pl.program_id(0)
    layer = place[2 * pieces]
    for i in range(4 * pieces):

        @pl.when((step == i % (2 * pieces)) & (layer == i // (2 * pieces)))
        def _(i=i):
            at = 0
            for out, width in zip(outs, widths):
                out[...] = ins[i][:, at : at + width].astype(F32)
                at += width


def assemble(place, arrays, widths):
    pieces = len(arrays) // 4
    rows, cols = arrays[0].shape
    tile = ROW_TILE
    while rows % tile:
        tile //= 2
    steps = rows // tile

    def in_map(i, step, t, place):
        chosen = (step == i % (2 * pieces)) & (place[2 * pieces] == i // (2 * pieces))
        return (jnp.where(chosen, t, jnp.where(step > i % (2 * pieces), steps - 1, 0)), 0)

    def out_map(step, t, place):
        return (place[step] * steps + t, 0)

    return pl.pallas_call(
        functools.partial(assemble_body, pieces, widths),
        out_shape=[jax.ShapeDtypeStruct((2 * pieces * rows, w), F32) for w in widths],
        grid_spec=pltpu.PrefetchScalarGridSpec(
            num_scalar_prefetch=1,
            grid=(2 * pieces, steps),
            in_specs=[
                pl.BlockSpec((tile, cols), functools.partial(in_map, i)) for i in range(4 * pieces)
            ],
            out_specs=[pl.BlockSpec((tile, w), out_map) for w in widths],
        ),
        compiler_params=pltpu.CompilerParams(vmem_limit_bytes=VMEM_BYTES),
        cost_estimate=pl.CostEstimate(
            flops=0, bytes_accessed=2 * pieces * rows * cols * 6, transcendentals=0
        ),
    )(place, *arrays)


def swap_cores(block):
    return lax.ppermute(block, "section", [(0, 1), (1, 0)])


def to_core(block, core):
    return lax.ppermute(block, "section", [(1 - core, core)])


def ring_step(block):
    count = lax.axis_size("mp")
    return lax.ppermute(block, "mp", [(i, (i + 1) % count) for i in range(count)])


def ring_gather(block):
    blocks = [block]
    for _ in range(lax.axis_size("mp") - 1):
        blocks.append(ring_step(blocks[-1]))
    return jnp.concatenate(blocks, axis=0)


def ring_sum(part):
    count = lax.axis_size("mp")
    rows = part.shape[0] // count
    running = part[rows : 2 * rows]
    for t in range(2, count):
        running = (
            ring_step(running).astype(F32) + part[t * rows : (t + 1) * rows].astype(F32)
        ).astype(LOW)
    return ring_step(running).astype(F32) + part[:rows].astype(F32)


def across_ctx(block, distance):
    count = lax.axis_size("ctx")
    return lax.ppermute(block, "ctx", [(i, i ^ distance) for i in range(count)])


def joint_step(block, t, bits):
    count = 1 << bits
    route = []
    for core in range(2):
        distance = 1 << (t if core == 0 else bits - 1 - t)
        route += [(core * count + i, core * count + (i ^ distance)) for i in range(count)]
    return lax.ppermute(block, ("section", "ctx"), route)


def row_norm(rows, gain):
    scaling = lax.rsqrt(jnp.mean(rows * rows, axis=-1, keepdims=True) + EPSILON)
    return rows * scaling * gain


def row_norm_back(rows, gain, grad):
    scaling = lax.rsqrt(jnp.mean(rows * rows, axis=-1, keepdims=True) + EPSILON)
    inner = grad * gain
    back = scaling * inner - rows * (
        scaling * scaling * scaling * jnp.mean(inner * rows, axis=-1, keepdims=True)
    )
    return back, jnp.sum(grad * rows * scaling, axis=0)


def attention_forward(attn_in, h_rows, weights, gains, tables):
    wq, wk, wv, w_out = weights[:4]
    cosine, sine, q_pos, k_pos = tables
    rows, width = attn_in.shape
    q_width, kv_width = wq.shape[1], wk.shape[1]
    n_ctx = lax.axis_size("ctx")
    shape = jax.ShapeDtypeStruct
    q_proj, k_proj, queries, kv = kernel_call(
        qkv_forward_body,
        [
            shape((rows, q_width), F32),
            shape((rows, kv_width), F32),
            shape((rows, q_width), LOW),
            shape((rows, 2 * kv_width), LOW),
        ],
        2 * rows * width * (q_width + 2 * kv_width),
        (attn_in, wq, wk, wv, gains["query"], gains["key"], cosine, sine),
    )
    blocks = [kv] + [across_ctx(kv, j) for j in range(1, n_ctx)]
    part, attended, log_total = kernel_call(
        functools.partial(attend_body, n_ctx),
        [
            shape((rows, width), LOW),
            shape((rows, q_width), LOW),
            shape((rows, q_width // HD), F32),
        ],
        2 * rows * q_width * (2 * rows * n_ctx + width),
        (queries, *blocks, q_pos, k_pos, w_out),
    )
    mid = h_rows + ring_sum(part)
    kept = {
        "attn_in": attn_in,
        "h_rows": h_rows,
        "q_proj": q_proj,
        "k_proj": k_proj,
        "queries": queries,
        "blocks": blocks,
        "attended": attended,
        "log_total": log_total,
        "mid": mid,
    }
    return mid, kept


def mlp_forward(mid, weights, gains):
    w_gate, w_up, w_down = weights[4:]
    mlp_in = ring_gather(row_norm(mid, gains["mlp"]).astype(LOW))
    gate = dot_nn(mlp_in, w_gate)
    up = dot_nn(mlp_in, w_up)
    hidden = (jax.nn.silu(gate) * up).astype(LOW)
    result = mid + ring_sum(dot_nn(hidden, w_down).astype(LOW))
    kept = {"mlp_in": mlp_in, "gate": gate.astype(LOW), "up": up.astype(LOW), "hidden": hidden}
    return result, kept


def mlp_backward(grad_out, branch, kept, weights, gains):
    w_gate, w_up, w_down = weights[4:]
    grad_hidden = dot_nt(branch, w_down)
    gate, up = kept["gate"].astype(F32), kept["up"].astype(F32)
    sig = jax.nn.sigmoid(gate)
    grad_gate = (grad_hidden * up * sig * (1.0 + gate * (1.0 - sig))).astype(LOW)
    grad_up = (grad_hidden * gate * sig).astype(LOW)
    part = (dot_nt(grad_gate, w_gate) + dot_nt(grad_up, w_up)).astype(LOW)
    back, grad_gain = row_norm_back(kept["mid"], gains["mlp"], ring_sum(part))
    return grad_out + back, grad_gain, jnp.concatenate([grad_gate, grad_up], axis=1)


def attention_backward(grad_mid, grad_rows, kept, weights, gains, tables):
    wq, wk, wv, w_out = weights[:4]
    cosine, sine, q_pos, k_pos = tables
    rows, width = grad_rows.shape
    q_width, kv_width = wq.shape[1], wk.shape[1]
    n_ctx = lax.axis_size("ctx")
    shape = jax.ShapeDtypeStruct
    grad_q, *grad_kv = kernel_call(
        functools.partial(attend_back_body, n_ctx),
        [shape((rows, q_width), F32)] + [shape((rows, 2 * kv_width), LOW)] * n_ctx,
        2 * rows * q_width * (5 * rows * n_ctx + width),
        (
            grad_rows,
            w_out,
            kept["queries"],
            *kept["blocks"],
            q_pos,
            k_pos,
            kept["attended"],
            kept["log_total"],
        ),
    )
    grad_kv = [grad_kv[0]] + [across_ctx(grad_kv[j], j) for j in range(1, n_ctx)]
    mixed, part, grad_q_gain, grad_k_gain = kernel_call(
        functools.partial(qkv_back_body, n_ctx),
        [
            shape((rows, q_width + 2 * kv_width), LOW),
            shape((rows, width), LOW),
            shape((1, HD), F32),
            shape((1, HD), F32),
        ],
        2 * rows * width * (q_width + 2 * kv_width),
        (
            grad_q,
            *grad_kv,
            kept["q_proj"],
            kept["k_proj"],
            gains["query"],
            gains["key"],
            cosine,
            sine,
            wq,
            wk,
            wv,
        ),
    )
    back, grad_gain = row_norm_back(kept["h_rows"], gains["attn"], ring_sum(part))
    return grad_mid + back, mixed, (grad_gain, grad_q_gain[0], grad_k_gain[0])


def core_bit(core, t, bits):
    shift = jnp.where(core == 0, t, bits - 1 - t)
    return (lax.axis_index("ctx") >> shift) & 1


def reduced_pieces(left, right):
    bits = lax.axis_size("ctx").bit_length() - 1
    core = lax.axis_index("section")
    half = left.shape[1] // 2

    def product(start, count):
        columns = lax.dynamic_slice_in_dim(left, start, count, axis=1)
        return dot_tn(columns, right)

    received = swap_cores(product((1 - core) * half, half).astype(LOW))
    count = half // 2
    flag = core_bit(core, 0, bits)

    def with_received(place):
        mine = product(core * half + place * count, count)
        other = lax.dynamic_slice_in_dim(received, place * count, count, axis=0)
        return mine + other.astype(F32)

    sent = joint_step(with_received(1 - flag).astype(LOW), 0, bits)
    total = with_received(flag) + sent.astype(F32)
    for t in range(1, bits):
        total = total.astype(LOW)
        count //= 2
        flag = core_bit(core, t, bits)
        sent = joint_step(
            lax.dynamic_slice_in_dim(total, (1 - flag) * count, count, axis=0), t, bits
        )
        total = (
            lax.dynamic_slice_in_dim(total, flag * count, count, axis=0).astype(F32)
            + sent.astype(F32)
        )
    pieces = [total.astype(LOW)]
    for t in reversed(range(bits)):
        pieces = pieces + [joint_step(piece, t, bits) for piece in pieces]
    return pieces


def piece_places(bits):
    core = lax.axis_index("section")
    places = []
    for owner in (core, 1 - core):
        mine = [core_bit(owner, t, bits) for t in range(bits)]
        for x in range(1 << bits):
            place = owner
            for t in range(bits):
                place = place * 2 + (mine[t] ^ ((x >> (bits - 1 - t)) & 1))
            places.append(place)
    return jnp.stack(places + [core]).astype(jnp.int32)


def home_rows(first_layer, second_layer):
    core = lax.axis_index("section")
    place = lax.axis_index("mp")
    count = lax.axis_size("mp")
    even = place % 2 == 0
    half = count // 2
    first_route = [(m, m // 2 if m % 2 == 0 else half + m // 2) for m in range(count)]
    second_route = [(m, half + m // 2 if m % 2 == 0 else m // 2) for m in range(count)]

    def across(route):
        return [(k * count + a, (1 - k) * count + b) for k in range(2) for a, b in route]

    def arranged(rows, move):
        low = [r.astype(LOW) for r in rows]
        one = move(jnp.where(even, low[0], low[1]), first_route)
        two = move(jnp.where(even, low[1], low[0]), second_route)
        lower = place < half
        return jnp.concatenate([jnp.where(lower, one, two), jnp.where(lower, two, one)], axis=0)

    pairs = list(zip(first_layer, second_layer))
    kept = arranged(
        [jnp.where(core == 0, a, b) for a, b in pairs],
        lambda block, route: lax.ppermute(block, "mp", route),
    )
    got = arranged(
        [jnp.where(core == 0, b, a) for a, b in pairs],
        lambda block, route: lax.ppermute(block, ("section", "mp"), across(route)),
    )
    return jnp.stack(
        [jnp.where(core == 0, kept, got), jnp.where(core == 0, got, kept)]
    ).astype(F32)


def shards(
    section_input,
    cotangent,
    pair_owner,
    attn_gain,
    w_query,
    w_key,
    w_value,
    query_gain,
    key_gain,
    w_output,
    mlp_gain,
    w_gate,
    w_up,
    w_down,
):
    n_ctx, n_mp = lax.axis_size("ctx"), lax.axis_size("mp")
    core, ctx, place = lax.axis_index("section"), lax.axis_index("ctx"), lax.axis_index("mp")
    is_first = core == 0
    width = section_input.shape[2]
    seq_rows = section_input.shape[1] * n_mp // SEQS
    own_rows = seq_rows // n_mp
    bits = n_ctx.bit_length() - 1

    def gathered(block):
        return lax.all_gather(block.astype(LOW), "mp", axis=0, tiled=True)

    raw = gathered(lax.dynamic_index_in_dim(section_input, core, 0, keepdims=False))
    top_grad = gathered(lax.dynamic_index_in_dim(cotangent, core, 0, keepdims=False))
    ring_order = (place - jnp.arange(n_mp, dtype=jnp.int32)) % n_mp

    def in_ring_order(rows, seq):
        return jnp.concatenate(
            [
                lax.dynamic_slice_in_dim(
                    rows, seq * seq_rows + ring_order[t] * own_rows, own_rows, axis=0
                )
                for t in range(n_mp)
            ],
            axis=0,
        )

    own = [w[0] for w in (w_query, w_key, w_value, w_output, w_gate, w_up, w_down)]
    other = [swap_cores(w) for w in own]
    own_gains = jnp.concatenate([attn_gain[0], mlp_gain[0], query_gain[0], key_gain[0]])
    other_gains = swap_cores(own_gains)
    layer_weights, layer_gains = [], []
    for layer in range(2):
        mine = is_first if layer == 0 else ~is_first
        layer_weights.append([jnp.where(mine, a, b) for a, b in zip(own, other)])
        flat = jnp.where(mine, own_gains, other_gains).astype(F32)
        layer_gains.append(
            {
                "attn": flat[:width],
                "mlp": flat[width : 2 * width],
                "query": flat[2 * width : 2 * width + HD][None],
                "key": flat[2 * width + HD :][None],
            }
        )

    owners = lax.dynamic_index_in_dim(pair_owner, core, 0, keepdims=False)
    index = (ring_order[:, None] * own_rows + jnp.arange(own_rows, dtype=jnp.int32)).reshape(-1)
    inv_freq = ROPE_BASE ** (-jnp.arange(0, HD, 2).astype(F32) / HD)
    seq_tables = []
    for seq in range(SEQS):
        block = jnp.take(owners[seq], ctx ^ jnp.arange(n_ctx, dtype=jnp.int32))[:, None]
        k_pos = jnp.where(
            index < STRETCH,
            block * STRETCH + index,
            (2 * n_ctx - 1 - block) * STRETCH + index - STRETCH,
        )
        q_pos = k_pos[0][:, None]
        angles = q_pos.astype(F32) * inv_freq[None, :]
        cosine, sine = jnp.cos(angles), jnp.sin(angles)
        seq_tables.append(
            (
                jnp.concatenate([cosine, cosine], axis=1),
                jnp.concatenate([-sine, sine], axis=1),
                q_pos,
                k_pos,
            )
        )

    raw_rows = [in_ring_order(raw, seq) for seq in range(SEQS)]
    h_rows = [rows[:own_rows].astype(F32) for rows in raw_rows]
    kept, outputs = [], []
    for layer in range(2):
        weights, gains = layer_weights[layer], layer_gains[layer]
        states, results = [], []
        for seq in range(SEQS):
            if layer == 0:
                attn_in = row_norm(raw_rows[seq].astype(F32), gains["attn"]).astype(LOW)
            else:
                attn_in = ring_gather(row_norm(h_rows[seq], gains["attn"]).astype(LOW))
            mid, state = attention_forward(attn_in, h_rows[seq], weights, gains, seq_tables[seq])
            result, more = mlp_forward(mid, weights, gains)
            states.append({**state, **more})
            results.append(result)
        kept.append(states)
        outputs.append(results)
        h_rows = results
    section_outputs = home_rows(outputs[0], outputs[1])

    branches = [in_ring_order(top_grad, seq) for seq in range(SEQS)]
    grads = [rows[:own_rows].astype(F32) for rows in branches]
    grads_in, gain_sums, pieces = [None, None], [None, None], [None, None]
    for layer in (1, 0):
        weights, gains = layer_weights[layer], layer_gains[layer]
        if layer == 0:
            branches = [ring_gather(g.astype(LOW)) for g in grads]
        states = kept[layer]

        def both(key):
            return jnp.concatenate([state[key] for state in states], axis=0)

        branch_all = jnp.concatenate(branches, axis=0)
        down = reduced_pieces(both("hidden"), branch_all)
        mids, grad_rows, grad_both, mlp_gains = [], [], [], []
        for seq in range(SEQS):
            grad_mid, gain_part, pair = mlp_backward(
                grads[seq], branches[seq], states[seq], weights, gains
            )
            mids.append(grad_mid)
            mlp_gains.append(gain_part)
            grad_both.append(pair)
            grad_rows.append(ring_gather(grad_mid.astype(LOW)))
        gate_up = reduced_pieces(both("mlp_in"), jnp.concatenate(grad_both, axis=0))
        out = reduced_pieces(both("attended"), jnp.concatenate(grad_rows, axis=0))
        mixed, attn_gains, results = [], [], []
        for seq in range(SEQS):
            grad_in, mix, gain_parts = attention_backward(
                mids[seq], grad_rows[seq], states[seq], weights, gains, seq_tables[seq]
            )
            results.append(grad_in)
            mixed.append(mix)
            attn_gains.append(gain_parts)
        qkv = reduced_pieces(both("attn_in"), jnp.concatenate(mixed, axis=0))
        pieces[layer] = (qkv, out, gate_up, down)
        gain_sums[layer] = jnp.concatenate(
            [
                attn_gains[0][0] + attn_gains[1][0],
                mlp_gains[0] + mlp_gains[1],
                attn_gains[0][1] + attn_gains[1][1],
                attn_gains[0][2] + attn_gains[1][2],
            ]
        )
        grads_in[layer] = results
        grads = results
    input_grads = home_rows(grads_in[0], grads_in[1])
    all_gains = lax.psum(jnp.stack(gain_sums), ("section", "ctx", "mp"))
    flat = lax.dynamic_index_in_dim(all_gains, core, 0, keepdims=False)

    places = piece_places(bits)
    q_width, kv_width, ff = w_query.shape[2], w_key.shape[2], w_gate.shape[2]
    widths = ((q_width, kv_width, kv_width), (width,), (ff, ff), (width,))
    laid = []
    for at in range(4):
        arrays = []
        for layer in range(2):
            arrays += pieces[layer][at]
            arrays += [to_core(piece, layer) for piece in pieces[layer][at]]
        laid.append([whole[None] for whole in assemble(places, arrays, widths[at])])
    (g_query, g_key, g_value), (g_output,), (g_gate, g_up), (g_down,) = laid
    return (
        section_outputs[None],
        input_grads[None],
        flat[:width][None],
        g_query,
        g_key,
        g_value,
        flat[2 * width : 2 * width + HD][None],
        flat[2 * width + HD :][None],
        g_output,
        flat[width : 2 * width][None],
        g_gate,
        g_up,
        g_down,
    )


def solution(mesh):
    in_specs = (
        P(None, ("ctx", "mp"), None),
        P(None, ("ctx", "mp"), None),
        P(),
        P("section", None),
        P("section", None, "mp"),
        P("section", None, "mp"),
        P("section", None, "mp"),
        P("section", None),
        P("section", None),
        P("section", "mp", None),
        P("section", None),
        P("section", None, "mp"),
        P("section", None, "mp"),
        P("section", "mp", None),
    )
    out_specs = (
        P("section", None, ("ctx", "mp"), None),
        P("section", None, ("ctx", "mp"), None),
        P("section", None),
        P("section", None, "mp"),
        P("section", None, "mp"),
        P("section", None, "mp"),
        P("section", None),
        P("section", None),
        P("section", "mp", None),
        P("section", None),
        P("section", None, "mp"),
        P("section", None, "mp"),
        P("section", "mp", None),
    )
    return jax.shard_map(shards, mesh=mesh, in_specs=in_specs, out_specs=out_specs, check_vma=False)
```

```python
import functools
from types import SimpleNamespace

import jax
import jax.numpy as jnp
from jax import lax
from jax.experimental import pallas as pl
from jax.experimental.pallas import tpu as pltpu
from jax.sharding import PartitionSpec as P

HD = 128
LANES = 128
MB = 2
SEQS = 2
STRETCH = 128
EPSILON = 1e-06
ROPE_BASE = 1000000.0
MASKED_SCORE = -1e30
SCALING = HD ** (-0.5)
LOW = jnp.bfloat16
F32 = jnp.float32
VMEM_SPARE = 12 * 1024 * 1024
VMEM_LEAST = 50 * 1024 * 1024


def dot_nn(left, right):
    return lax.dot_general(left, right, (((1,), (0,)), ((), ())), preferred_element_type=F32)


def dot_nt(left, right):
    return lax.dot_general(left, right, (((1,), (1,)), ((), ())), preferred_element_type=F32)


def dot_tn(left, right):
    return lax.dot_general(left, right, (((0,), (0,)), ((), ())), preferred_element_type=F32)


def kernel_call(body, out_shape, flops, args, layer, weights):
    held = [jax.ShapeDtypeStruct(x.shape, x.dtype) for x in (*args, *[w[0] for w in weights])]
    moved = sum(x.size * x.dtype.itemsize for x in (*held, *out_shape))
    n_args, n_weights, n_out = len(args), len(weights), len(out_shape)

    def whole(*refs):
        ins, rest = refs[:n_args], refs[n_args:]
        pairs, rest = rest[: 2 * n_weights], rest[2 * n_weights :]
        outs, here, sems = rest[:n_out], rest[n_out:-1], rest[-1]
        home = lax.axis_index(CORES) == layer

        def copy(i, source):
            return pltpu.make_async_copy(source, here[i], sems.at[i])

        for i, ref in enumerate(ins):
            copy(i, ref).start()
        for which, taken in ((0, home), (1, jnp.logical_not(home))):

            @pl.when(taken)
            def _(which=which):
                for i in range(n_weights):
                    copy(n_args + i, pairs[2 * i + which]).start()

        def arrived(i):
            copy(n_args + i, pairs[2 * i]).wait()
            return here[n_args + i]

        for i, ref in enumerate(ins):
            copy(i, ref).wait()
        gets = [functools.partial(arrived, i) for i in range(n_weights)]
        body(*here[:n_args], *gets, *outs)

    vmem, hbm = pl.BlockSpec(memory_space=pltpu.VMEM), pl.BlockSpec(memory_space=pltpu.HBM)
    return pl.pallas_call(
        whole,
        out_shape=out_shape,
        in_specs=[hbm] * (n_args + 2 * n_weights),
        out_specs=[vmem] * n_out,
        scratch_shapes=[pltpu.VMEM(x.shape, x.dtype) for x in held]
        + [pltpu.SemaphoreType.DMA((len(held),))],
        compiler_params=pltpu.CompilerParams(vmem_limit_bytes=max(moved + VMEM_SPARE, VMEM_LEAST)),
        cost_estimate=pl.CostEstimate(flops=flops, bytes_accessed=moved, transcendentals=0),
    )(*args, *[ref for w in weights for ref in w])


def qkv_forward_body(q_width, x, gains, turns, get_qkv, proj, queries, kv):
    cos_full, sin_signed = turns[:, :HD], turns[:, HD:]

    def prepared(head, gain):
        scaling = lax.rsqrt(jnp.mean(head * head, axis=-1, keepdims=True) + EPSILON)
        normed = head * scaling * gain
        return (normed * cos_full + pltpu.roll(normed, HD // 2, 1) * sin_signed).astype(LOW)

    mixed = dot_nn(x[...], get_qkv()[...])
    both = proj.shape[1]
    proj[...] = mixed[:, :both]
    for at in range(0, q_width, HD):
        queries[:, at : at + HD] = prepared(mixed[:, at : at + HD], gains[:1, :])
    for at in range(q_width, both, HD):
        kv[:, at - q_width : at - q_width + HD] = prepared(mixed[:, at : at + HD], gains[1:, :])
    kv[:, both - q_width :] = mixed[:, both:].astype(LOW)


def mlp_forward_body(x, get_gate, get_up, get_down, gate, up, hidden, *parts):
    rows = x[...]
    gate_all = dot_nn(rows, get_gate()[...])
    up_all = dot_nn(rows, get_up()[...])
    gate[...] = gate_all.astype(LOW)
    up[...] = up_all.astype(LOW)
    hidden[...] = (jax.nn.silu(gate_all) * up_all).astype(LOW)
    store_product(parts, hidden[...], get_down(), dot_nn)


def mlp_back_body(branch, gate, up, get_down, get_gate, get_up, grad_gate, grad_up, *parts):
    grad_hidden = dot_nt(branch[...], get_down()[...])
    gate_all, up_all = gate[...].astype(F32), up[...].astype(F32)
    sig = jax.nn.sigmoid(gate_all)
    grad_gate[...] = (grad_hidden * up_all * sig * (1.0 + gate_all * (1.0 - sig))).astype(LOW)
    grad_up[...] = (grad_hidden * gate_all * sig).astype(LOW)
    w_gate, w_up = get_gate(), get_up()
    for at in range(0, w_gate.shape[0], 512):
        here = pl.ds(at, 512)
        total = dot_nt(grad_gate[...], w_gate[here, :]) + dot_nt(grad_up[...], w_up[here, :])
        store_columns(parts, here, total)


def store_columns(parts, here, rows):
    size = parts[0].shape[0]
    for i, part in enumerate(parts):
        part[:, here] = rows[i * size : (i + 1) * size].astype(LOW)


def store_product(parts, rows, weight, dot):
    for at in range(0, weight.shape[1], 512):
        here = pl.ds(at, 512)
        store_columns(parts, here, dot(rows, weight[:, here]))


def store_blocks(parts, rows):
    size = parts[0].shape[0]
    for i, part in enumerate(parts):
        part[...] = rows[i * size : (i + 1) * size].astype(LOW)


def attend_body(n_ctx, queries, *refs):
    blocks = refs[:n_ctx]
    q_pos, k_pos, get_out = refs[n_ctx : n_ctx + 3]
    attended, log_total, *parts = refs[n_ctx + 3 :]
    rows = queries.shape[0]
    kv_width = blocks[0].shape[1] // 2
    groups = queries.shape[1] // kv_width
    place = jnp.concatenate([q_pos[...]] * groups, axis=0)
    for kv_head in range(kv_width // HD):
        first = kv_head * groups
        stacked = jnp.concatenate(
            [queries[:, (first + i) * HD : (first + i + 1) * HD] for i in range(groups)], axis=0
        )
        at = kv_head * HD
        scores = []
        for j, block in enumerate(blocks):
            raw = dot_nt(stacked, block[:, at : at + HD]) * SCALING
            scores.append(jnp.where(k_pos[j : j + 1, :] <= place, raw, MASKED_SCORE))
        top = functools.reduce(
            jnp.maximum, [jnp.max(s, axis=1, keepdims=True) for s in scores]
        )
        total, running = 0.0, 0.0
        for s, block in zip(scores, blocks):
            weights = jnp.exp(s - top)
            total = total + jnp.sum(weights, axis=1, keepdims=True)
            running = running + dot_nn(
                weights.astype(LOW), block[:, kv_width + at : kv_width + at + HD]
            )
        result = (running / total).astype(LOW)
        logs = top + jnp.log(total)
        for i in range(groups):
            head = first + i
            attended[:, head * HD : (head + 1) * HD] = result[i * rows : (i + 1) * rows]
            log_total[:, head : head + 1] = logs[i * rows : (i + 1) * rows]
    store_blocks(parts, dot_nn(attended[...], get_out()[...]))


def attend_back_body(n_ctx, grad_rows, queries, *refs):
    blocks = refs[:n_ctx]
    q_pos, k_pos, attended, log_total, get_out, grad_q = refs[n_ctx : n_ctx + 6]
    grad_kv = refs[n_ctx + 6 :]
    rows = queries.shape[0]
    kv_width = blocks[0].shape[1] // 2
    groups = queries.shape[1] // kv_width
    grad_all = dot_nt(grad_rows[...], get_out()[...]).astype(LOW)
    place = jnp.concatenate([q_pos[...]] * groups, axis=0)
    for kv_head in range(kv_width // HD):
        heads = [kv_head * groups + i for i in range(groups)]
        stacked = jnp.concatenate([queries[:, h * HD : (h + 1) * HD] for h in heads], axis=0)
        grads = jnp.concatenate([grad_all[:, h * HD : (h + 1) * HD] for h in heads], axis=0)
        out_low = jnp.concatenate([attended[:, h * HD : (h + 1) * HD] for h in heads], axis=0)
        logs = jnp.concatenate([log_total[:, h : h + 1] for h in heads], axis=0)
        delta = jnp.sum(grads.astype(F32) * out_low.astype(F32), axis=1, keepdims=True)
        at = kv_head * HD
        total = 0.0
        for j, block in enumerate(blocks):
            keys = block[:, at : at + HD]
            values = block[:, kv_width + at : kv_width + at + HD]
            shifted = dot_nt(stacked, keys) * SCALING - logs
            probs = jnp.exp(jnp.where(k_pos[j : j + 1, :] <= place, shifted, MASKED_SCORE))
            grad_scores = (probs * (dot_nt(grads, values) - delta)).astype(LOW)
            total = total + dot_nn(grad_scores, keys)
            grad_kv[j][:, at : at + HD] = (dot_tn(grad_scores, stacked) * SCALING).astype(LOW)
            grad_kv[j][:, kv_width + at : kv_width + at + HD] = dot_tn(
                probs.astype(LOW), grads
            ).astype(LOW)
        for i, h in enumerate(heads):
            grad_q[:, h * HD : (h + 1) * HD] = total[i * rows : (i + 1) * rows] * SCALING


def qkv_back_body(n_ctx, grad_q, *refs):
    grad_kv = refs[:n_ctx]
    proj, gains, turns, get_qkv, mixed, grad_gains, *parts = refs[n_ctx:]
    cos_full, sin_signed = turns[:, :HD], turns[:, HD:]
    q_width = grad_q.shape[1]
    kv_width = proj.shape[1] - q_width

    def pulled(grad, head, gain):
        turned = grad * cos_full + pltpu.roll(grad * sin_signed, HD // 2, 1)
        scaling = lax.rsqrt(jnp.mean(head * head, axis=-1, keepdims=True) + EPSILON)
        inner = turned * gain
        back = scaling * inner - head * (
            scaling * scaling * scaling * jnp.mean(inner * head, axis=-1, keepdims=True)
        )
        return back.astype(LOW), jnp.sum(turned * head * scaling, axis=0, keepdims=True)

    total = 0.0
    for at in range(0, q_width, HD):
        back, gain_part = pulled(grad_q[:, at : at + HD], proj[:, at : at + HD], gains[:1, :])
        mixed[:, at : at + HD] = back
        total = total + gain_part
    grad_gains[:1, :] = total
    summed = functools.reduce(jnp.add, [g[...].astype(F32) for g in grad_kv])
    total = 0.0
    for at in range(0, kv_width, HD):
        here = slice(q_width + at, q_width + at + HD)
        back, gain_part = pulled(summed[:, at : at + HD], proj[:, here], gains[1:, :])
        mixed[:, here] = back
        total = total + gain_part
    grad_gains[1:, :] = total
    mixed[:, q_width + kv_width :] = summed[:, kv_width:].astype(LOW)
    w_qkv = get_qkv()
    for at in range(0, w_qkv.shape[0], 512):
        here = pl.ds(at, 512)
        store_columns(parts, here, dot_nt(mixed[...], w_qkv[here, :]))


def product_body(n_left, n_right, place, *refs):
    lefts, refs = refs[:n_left], refs[n_left:]
    groups = []
    for count in n_right:
        groups.append(refs[:count])
        refs = refs[count:]
    *extra, out, left_all, right_all, sems = refs
    tile, rows = out.shape[0], left_all.shape[1]
    step = pl.program_id(0)

    @pl.when(step == 0)
    def _():
        copies = []
        row = 0
        for ref in lefts:
            source = ref.at[:, pl.ds(pl.multiple_of(place[0] * rows, rows), rows)]
            copies.append((source, left_all.at[pl.ds(row, ref.shape[0]), :]))
            row += ref.shape[0]
        column = 0
        for group in groups:
            row = 0
            for ref in group:
                here = (pl.ds(row, ref.shape[0]), pl.ds(column, ref.shape[1]))
                copies.append((ref, right_all.at[here]))
                row += ref.shape[0]
            column += group[0].shape[1]
        copies = [
            pltpu.make_async_copy(source, target, sems.at[i])
            for i, (source, target) in enumerate(copies)
        ]
        for copy in copies:
            copy.start()
        for copy in copies:
            copy.wait()

    left = left_all[:, pl.ds(pl.multiple_of(step * tile, tile), tile)]
    width = 512
    for at in range(0, out.shape[1], width):
        result = dot_tn(left, right_all[:, at : at + width])
        if extra:
            result = result + extra[0][:, at : at + width].astype(F32)
        out[:, at : at + width] = result.astype(LOW)


def piece_product(pieces, which, lefts, rights, extra=None, extra_at=0):
    depth = sum(x.shape[0] for x in lefts)
    rows = lefts[0].shape[1] // pieces
    cols = sum(group[0].shape[1] for group in rights)
    tile = 256
    while rows % tile:
        tile //= 2
    steps = rows // tile
    flat = [x for group in rights for x in group]
    extras = [] if extra is None else [extra]
    place = jnp.stack([jnp.asarray(which, jnp.int32), jnp.asarray(extra_at, jnp.int32)])
    held = 2 * depth * (rows + cols)
    return pl.pallas_call(
        functools.partial(product_body, len(lefts), [len(group) for group in rights]),
        out_shape=jax.ShapeDtypeStruct((rows, cols), LOW),
        grid_spec=pltpu.PrefetchScalarGridSpec(
            num_scalar_prefetch=1,
            grid=(steps,),
            in_specs=[pl.BlockSpec(memory_space=pltpu.HBM)] * (len(lefts) + len(flat))
            + [
                pl.BlockSpec((tile, cols), lambda i, place: (place[1] * steps + i, 0))
                for _ in extras
            ],
            out_specs=pl.BlockSpec((tile, cols), lambda i, place: (i, 0)),
            scratch_shapes=[
                pltpu.VMEM((depth, rows), LOW),
                pltpu.VMEM((depth, cols), LOW),
                pltpu.SemaphoreType.DMA((len(lefts) + len(flat),)),
            ],
        ),
        compiler_params=pltpu.CompilerParams(
            vmem_limit_bytes=max(held + 8 * tile * cols + VMEM_SPARE, VMEM_LEAST)
        ),
        cost_estimate=pl.CostEstimate(
            flops=2 * depth * rows * cols,
            bytes_accessed=held + 2 * rows * cols * (1 + len(extras)),
            transcendentals=0,
        ),
    )(place, *lefts, *flat, *extras)


def assemble_body(widths, place, *refs):
    ins, outs = refs[:4], refs[4:]
    step = pl.program_id(0)
    for i in range(4):

        @pl.when((step == i % 2) & (place[0] == i // 2))
        def _(i=i):
            at = 0
            for out, width in zip(outs, widths):
                out[...] = ins[i][:, at : at + width].astype(F32)
                at += width


def assemble(place, arrays, widths):
    rows, cols = arrays[0].shape
    tile = 128
    while rows % tile:
        tile //= 2
    steps = rows // tile

    def in_map(i, step, t, place):
        wanted = place[0] == i // 2
        if i % 2 == 0:
            moving = jnp.where(step == 0, t, steps - 1)
        else:
            moving = jnp.where(step == 0, 0, t)
        return (jnp.where(wanted, moving, 0), 0)

    def out_map(step, t, place):
        return ((place[0] ^ step) * steps + t, 0)

    return pl.pallas_call(
        functools.partial(assemble_body, widths),
        out_shape=[jax.ShapeDtypeStruct((2 * rows, w), F32) for w in widths],
        grid_spec=pltpu.PrefetchScalarGridSpec(
            num_scalar_prefetch=1,
            grid=(2, steps),
            in_specs=[pl.BlockSpec((tile, cols), functools.partial(in_map, i)) for i in range(4)],
            out_specs=[pl.BlockSpec((tile, w), out_map) for w in widths],
        ),
        compiler_params=pltpu.CompilerParams(vmem_limit_bytes=24 * tile * cols + VMEM_SPARE),
        cost_estimate=pl.CostEstimate(
            flops=0, bytes_accessed=2 * rows * cols * 6, transcendentals=0
        ),
    )(place, *arrays)


Z_SLOT, Z_HOP = 5.5, 3.2


START_COST = 0.9
AHEAD = 10.0
RING, LINKS, SWAP, SPARSE, NONE = range(5)
RAW, TOP, OUTPUT, INPUT_GRAD, GAIN, GAINS, HALF, WHOLE, HOME, GATE_UP, DOWN, OUT, QKV = range(13)
CORES, CTX, MP = "section", "ctx", "mp"


class Send:
    def __init__(self, kind, blocks, span, then=0.0, slack=0.0):
        self.kind, self.blocks, self.span, self.then, self.slack = kind, blocks, span, then, slack


class Need:
    def __init__(self, *keys, then=0.0):
        self.keys, self.then = keys, then


class Wait:
    def __init__(self, until):
        self.until = until


class Lane:
    def __init__(self, work, rank, name, patience):
        self.work, self.rank, self.name, self.patience = work, rank, name, patience
        self.ready, self.value, self.wanted, self.then = 0.0, None, None, 0.0


class Driver:
    def __init__(self, token):
        self.token, self.now, self.cost = token, 0.0, 0.0
        self.lanes, self.store, self.log = [], {}, []
        self.free = [0.0] * 5

    def spend(self, cost):
        self.cost += cost

    def put(self, key, value):
        self.store[key] = (self.now + self.cost, value)

    def add(self, work, rank, name=None, patience=3.0):
        lane = Lane(work, rank, name, patience)
        lane.ready = self.now
        self.lanes.append(lane)

    def tied(self, value):
        leaves, tree = jax.tree.flatten(value)
        if not leaves:
            return value
        *leaves, _ = lax.optimization_barrier((*leaves, self.token))
        return jax.tree.unflatten(tree, leaves)

    def turn(self):
        while self.free[LINKS] > self.now + AHEAD:
            yield Wait(self.free[LINKS] - AHEAD)

    def ready_at(self, lane):
        if lane.wanted is None:
            return lane.ready
        if any(key not in self.store for key in lane.wanted):
            return None
        return max([lane.ready] + [self.store[key][0] for key in lane.wanted])

    def step(self, lane):
        self.log.append((self.now, self.ready_at(lane), lane.name))
        self.now = max(self.now, self.ready_at(lane))
        if lane.wanted is not None:
            lane.value = tuple(self.store[key][1] for key in lane.wanted)
            lane.wanted = None
        self.cost = 0.0
        value = None if lane.value is None else self.tied(lane.value)
        lane.value = None
        try:
            request = lane.work.send(value)
        except StopIteration:
            self.lanes.remove(lane)
            self.now += self.cost
            return
        self.now += self.cost
        if isinstance(request, Wait):
            lane.ready = max(self.now, request.until)
            return
        lane.then = request.then
        if isinstance(request, Need):
            lane.wanted, lane.ready = request.keys, self.now
            return
        self.now += START_COST * len(request.blocks)
        start = max(self.now, self.free[request.kind])
        self.free[request.kind] = start + request.span
        lane.ready = start + request.span + Z_HOP + request.slack
        lane.value = [move(block) for move, block in request.blocks]
        self.token = request.blocks[0][1]

    def run(self):
        while self.lanes:
            times = [(self.ready_at(lane), lane) for lane in self.lanes]
            times = [(at, lane) for at, lane in times if at is not None]
            main = [pair for pair in times if pair[1].rank == 0]
            soon = min([at for at, _ in main], default=1e9)
            waiting = [
                (at, lane)
                for at, lane in times
                if at <= self.now
                and (lane.rank == 0 or max(self.now, at) + lane.then <= soon + lane.patience)
            ]
            if waiting:
                lane = min(waiting, key=lambda pair: (pair[1].rank, pair[0]))[1]
            elif main:
                lane = min(
                    [p for p in times if p[1].rank == 0 or p[0] + p[1].then <= soon + p[1].patience],
                    key=lambda pair: (pair[0], pair[1].rank),
                )[1]
            else:
                lane = min(times, key=lambda pair: (pair[0], pair[1].rank))[1]
            self.step(lane)


def swap_cores(block):
    return lax.ppermute(block, CORES, [(0, 1), (1, 0)])


def to_core(core):
    return lambda block: lax.ppermute(block, CORES, [(1 - core, core)])


def ring_step(block):
    count = lax.axis_size(MP)
    return lax.ppermute(block, MP, [(i, (i + 1) % count) for i in range(count)])


def across_ctx(distance):
    count = lax.axis_size(CTX)
    return lambda block: lax.ppermute(block, CTX, [(i, i ^ distance) for i in range(count)])


def ring_gather(driver, block):
    blocks = [block]
    for _ in range(lax.axis_size(MP) - 1):
        (block,) = yield Send(RING, [(ring_step, block)], Z_SLOT)
        blocks.append(block)
    driver.spend(1.5)
    return lax.optimization_barrier(jnp.concatenate(blocks, axis=0))


def ring_sum(driver, part):
    count = lax.axis_size(MP)
    if not isinstance(part, list):
        rows = part.shape[0] // count
        part = [part[t * rows : (t + 1) * rows] for t in range(count)]
        driver.spend(0.8)
    running = part[1]
    for t in range(2, count):
        (got,) = yield Send(RING, [(ring_step, running)], Z_SLOT)
        running = (got.astype(F32) + part[t].astype(F32)).astype(LOW)
        driver.spend(1.4)
    (got,) = yield Send(RING, [(ring_step, running)], Z_SLOT)
    driver.spend(1.4)
    return got.astype(F32) + part[0].astype(F32)


def ctx_exchange(blocks, span=12.0):
    moves = [(across_ctx(j + 1), block) for j, block in enumerate(blocks)]
    got = yield Send(LINKS, moves, span)
    return got


def summed_everywhere(driver, block):
    for axis in (MP, CORES, CTX):
        count = lax.axis_size(axis)
        distance = 1
        while distance < count:
            route = [(i, i ^ distance) for i in range(count)]
            (got,) = yield Send(
                LINKS if axis == CTX else NONE,
                [(functools.partial(lax.ppermute, axis_name=axis, perm=route), block)],
                2.0,
                1.0,
                5.0,
            )
            block = block + got
            driver.spend(1.0)
            distance *= 2
    return block


def row_norm(rows, gain):
    scaling = lax.rsqrt(jnp.mean(rows * rows, axis=-1, keepdims=True) + EPSILON)
    return rows * scaling * gain


def row_norm_back(rows, gain, grad):
    scaling = lax.rsqrt(jnp.mean(rows * rows, axis=-1, keepdims=True) + EPSILON)
    inner = grad * gain
    back = scaling * inner - rows * (
        scaling * scaling * scaling * jnp.mean(inner * rows, axis=-1, keepdims=True)
    )
    return back, jnp.sum(grad * rows * scaling, axis=0)


def shape(rows, cols, kind=LOW):
    return jax.ShapeDtypeStruct((rows, cols), kind)


def part_shapes(rows, width):
    count = lax.axis_size(MP)
    return [shape(rows // count, width)] * count


def project(attn_in, layer, weights, gains, tables):
    turns, q_pos, k_pos = tables
    rows, width = attn_in.shape
    total = weights.qkv[0].shape[1]
    q_width = weights.output[0].shape[0]
    kv_width = (total - q_width) // 2
    return kernel_call(
        functools.partial(qkv_forward_body, q_width),
        [shape(rows, q_width + kv_width, F32), shape(rows, q_width), shape(rows, 2 * kv_width)],
        2 * rows * width * total,
        (attn_in, gains.heads, turns),
        layer,
        [weights.qkv],
    )


def attend(queries, blocks, layer, weights, tables):
    turns, q_pos, k_pos = tables
    rows, q_width = queries.shape
    width = weights.output[0].shape[1]
    attended, log_total, *parts = kernel_call(
        functools.partial(attend_body, len(blocks)),
        [shape(rows, q_width), shape(rows, q_width // HD, F32)] + part_shapes(rows, width),
        2 * rows * q_width * (2 * rows * len(blocks) + width),
        (queries, *blocks, q_pos, k_pos),
        layer,
        [weights.output],
    )
    return parts, attended, log_total


def mlp_forward(mlp_in, layer, weights):
    ff = weights.gate[0].shape[1]
    picked = [weights.gate, weights.up, weights.down]
    rows, width = mlp_in.shape
    gate, up, hidden, *parts = kernel_call(
        mlp_forward_body,
        [shape(rows, ff)] * 3 + part_shapes(rows, width),
        6 * rows * width * ff,
        (mlp_in,),
        layer,
        picked,
    )
    return gate, up, hidden, parts


def mlp_back(branch, kept, layer, weights):
    ff = weights.gate[0].shape[1]
    picked = [weights.down, weights.gate, weights.up]
    rows, width = branch.shape
    grad_gate, grad_up, *parts = kernel_call(
        mlp_back_body,
        [shape(rows, ff)] * 2 + part_shapes(rows, width),
        6 * rows * width * ff,
        (branch, kept.gate, kept.up),
        layer,
        picked,
    )
    return grad_gate, grad_up, parts


def attend_back(grad_rows, kept, layer, weights, tables):
    turns, q_pos, k_pos = tables
    blocks = kept.blocks
    rows, q_width = kept.queries.shape
    return kernel_call(
        functools.partial(attend_back_body, len(blocks)),
        [shape(rows, q_width, F32)] + [shape(*blocks[0].shape)] * len(blocks),
        2 * rows * q_width * (5 * rows * len(blocks) + grad_rows.shape[1]),
        (
            grad_rows,
            kept.queries,
            *blocks,
            q_pos,
            k_pos,
            kept.attended,
            kept.log_total,
        ),
        layer,
        [weights.output],
    )


def project_back(grad_q, grad_kv, kept, layer, weights, gains, tables):
    turns, q_pos, k_pos = tables
    rows, width = kept.attn_in.shape
    total = weights.qkv[0].shape[1]
    mixed, grad_gains, *parts = kernel_call(
        functools.partial(qkv_back_body, len(grad_kv)),
        [shape(rows, total), shape(2, HD, F32)] + part_shapes(rows, width),
        2 * rows * width * total,
        (grad_q, *grad_kv, kept.proj, gains.heads, turns),
        layer,
        [weights.qkv],
    )
    return mixed, parts, grad_gains


def sequence_lane(driver, seq, weights, gains, tables, own_rows, in_ring_order):
    (raw,) = yield Need(RAW)
    rows = in_ring_order(raw, seq)
    h_rows = rows[:own_rows].astype(F32)
    kept = []
    for layer in range(2):
        gain = gains[layer]
        if layer == 0:
            attn_in = row_norm(rows.astype(F32), gain.attn).astype(LOW)
            driver.spend(4.0)
        else:
            attn_in = yield from ring_gather(driver, row_norm(h_rows, gain.attn).astype(LOW))
        proj, queries, kv = project(attn_in, layer, weights, gain, tables)
        driver.spend(6.0)
        others = yield from ctx_exchange([kv] * (lax.axis_size(CTX) - 1))
        blocks = [kv] + others
        part, attended, log_total = attend(queries, blocks, layer, weights, tables)
        driver.spend(6.0)
        mid = h_rows + (yield from ring_sum(driver, part))
        driver.spend(1.0)
        mlp_in = yield from ring_gather(driver, row_norm(mid, gain.mlp).astype(LOW))
        gate, up, hidden, part = mlp_forward(mlp_in, layer, weights)
        driver.spend(9.5)
        kept.append(
            SimpleNamespace(
                attn_in=attn_in,
                h_rows=h_rows,
                proj=proj,
                queries=queries,
                blocks=blocks,
                attended=attended,
                log_total=log_total,
                mid=mid,
                mlp_in=mlp_in,
                gate=gate,
                up=up,
                hidden=hidden,
            )
        )
        h_rows = mid + (yield from ring_sum(driver, part))
        driver.spend(1.0)
        driver.put((OUTPUT, layer, seq), h_rows)

    (top_grad,) = yield Need(TOP)
    branch = in_ring_order(top_grad, seq)
    driver.spend(2.0)
    grad_out = branch[:own_rows].astype(F32)
    for layer in (1, 0):
        gain, state = gains[layer], kept[layer]
        if layer == 0:
            branch = yield from ring_gather(driver, grad_out.astype(LOW))
        driver.put((DOWN, layer, seq), (state.hidden, branch))
        grad_gate, grad_up, part = mlp_back(branch, state, layer, weights)
        driver.spend(12.0)
        driver.put((GATE_UP, layer, seq), (state.mlp_in, grad_gate, grad_up))
        back, mlp_gain = row_norm_back(
            state.mid, gain.mlp, (yield from ring_sum(driver, part))
        )
        driver.spend(4.0)
        grad_mid = grad_out + back
        grad_rows = yield from ring_gather(driver, grad_mid.astype(LOW))
        driver.put((OUT, layer, seq), (state.attended, grad_rows))
        grad_q, *grad_kv = attend_back(grad_rows, state, layer, weights, tables)
        driver.spend(10.0)
        grad_kv = [grad_kv[0]] + (yield from ctx_exchange(grad_kv[1:], 17.0))
        mixed, part, head_gains = project_back(
            grad_q, grad_kv, state, layer, weights, gain, tables
        )
        driver.spend(9.0)
        driver.put((QKV, layer, seq), (state.attn_in, mixed))
        back, attn_gain = row_norm_back(
            state.h_rows, gain.attn, (yield from ring_sum(driver, part))
        )
        driver.spend(4.0)
        grad_out = grad_mid + back
        driver.put((INPUT_GRAD, layer, seq), grad_out)
        driver.put(
            (GAIN, layer, seq), jnp.concatenate([attn_gain, mlp_gain, head_gains.reshape(-1)])
        )


def core_bit(t, bits):
    shift = jnp.where(lax.axis_index(CORES) == 0, t, bits - 1 - t)
    return (lax.axis_index(CTX) >> shift) & 1


def joint_step(t, bits):
    count = 1 << bits
    route = []
    for core in range(2):
        distance = 1 << (t if core == 0 else bits - 1 - t)
        route += [(core * count + i, core * count + (i ^ distance)) for i in range(count)]
    return lambda block: lax.ppermute(block, (CORES, CTX), route)


def sum_by_halving(driver, product, rows, cost, slack):
    core = lax.axis_index(CORES)
    bits = lax.axis_size(CTX).bit_length() - 1
    flag = core_bit(0, bits)
    sent = None
    if rows % (4 * LANES) == 0:
        sent = product(4, 2 * core + 1 - flag, 1 - flag)
        total = product(4, 2 * core + flag, flag)
    else:
        total = product(2, core, 0)
    driver.spend(cost * 1.4)
    for t in range(bits):
        if sent is None:
            flag, count = core_bit(t, bits), total.shape[0] // 2
            sent = lax.dynamic_slice_in_dim(total, (1 - flag) * count, count, axis=0)
            total = lax.dynamic_slice_in_dim(total, flag * count, count, axis=0)
            driver.spend(1.5 + sent.size * 2 / 1e6)
        size = sent.size * 2 / 1e6
        (got,) = yield Send(
            LINKS, [(joint_step(t, bits), sent)], 11.5 * size, 1.5 + size, slack + 6.0 * size
        )
        driver.spend(1.0 + size)
        total = (total.astype(F32) + got.astype(F32)).astype(LOW)
        sent = None
    for t in reversed(range(bits)):
        size = total.size * 2 / 1e6
        (got,) = yield Send(
            LINKS, [(joint_step(t, bits), total)], 11.5 * size, 1.5 + 2 * size, slack + 6.0 * size
        )
        flag = core_bit(t, bits) == 0
        total = jnp.concatenate(
            [jnp.where(flag, total, got), jnp.where(flag, got, total)], axis=0
        )
        driver.spend(1.5 + 2 * size)
    return total


def scattered(driver, product, cost, crowding):
    total = product(2, lax.axis_index(CORES), 0)
    driver.spend(cost * 1.2)
    move = functools.partial(lax.psum_scatter, axis_name=CTX, scatter_dimension=0, tiled=True)
    span = (13 + 2e-5 * total.size) * crowding
    (share,) = yield Send(SPARSE, [(move, total)], span, 1.0)
    return share, span


def sum_by_collectives(driver, product, rows, cost, slack):
    share, span = yield from scattered(driver, product, cost, 1.0)
    move = functools.partial(lax.all_gather, axis_name=CTX, axis=0, tiled=True)
    (total,) = yield Send(SPARSE, [(move, share)], span, 1.0)
    return total


def sum_by_both(driver, product, rows, cost, slack):
    if lax.axis_size(CTX) != 4:
        return (yield from sum_by_collectives(driver, product, rows, cost, slack))
    share, _ = yield from scattered(driver, product, cost, 1.35)
    first = lax.axis_index(CORES) == 0
    size = share.size * 2 / 1e6
    (got,) = yield Send(
        LINKS, [(joint_step(0, 2), share)], 11.5 * size, 1.5 + 2 * size, slack + 3.0 * size
    )
    flag = core_bit(0, 2) == 0
    pair = jnp.stack([jnp.where(flag, share, got), jnp.where(flag, got, share)])
    driver.spend(1.5 + 2 * size)
    (got,) = yield Send(
        LINKS, [(joint_step(1, 2), pair)], 23.0 * size, 2.0 + 4 * size, slack + 6.0 * size
    )
    flag = core_bit(1, 2) == 0
    low, high = jnp.where(flag, pair, got), jnp.where(flag, got, pair)
    driver.spend(2.0 + 4 * size)
    return jnp.concatenate(
        [
            low[0],
            jnp.where(first, low[1], high[0]),
            jnp.where(first, high[0], low[1]),
            high[1],
        ],
        axis=0,
    )


def matrix_lane(driver, name, layer, cost, way):
    parts = yield Need(*[(name, layer, seq) for seq in range(SEQS)], then=cost)
    lefts = [part[0] for part in parts]
    rights = [[part[at] for part in parts] for at in range(1, len(parts[0]))]
    driver.spend(cost)
    away = piece_product(2, 1 - lax.axis_index(CORES), lefts, rights)
    size = away.size * 2 / 1e6
    (received,) = yield Send(SWAP, [(swap_cores, away)], 2.0 + 1.6 * size, cost * 1.3, 4.0)

    def product(pieces, which, extra_at):
        return piece_product(pieces, which, lefts, rights, received, extra_at)

    slack = 4.0 if layer == 0 else 25.0
    half = yield from way(driver, product, lefts[0].shape[1], cost, slack)
    (other,) = yield Send(SWAP, [(to_core(layer), half)], 2.0 + 1.6 * size, 0.0, 4.0)
    driver.token = other
    driver.put((HALF, name, layer), (half, other))


def assemble_lane(driver, name, widths):
    first, second = yield Need((HALF, name, 0), (HALF, name, 1))
    core = lax.axis_index(CORES).astype(jnp.int32).reshape(1)
    whole = assemble(core, [*first, *second], widths)
    driver.token = whole[0]
    driver.put((WHOLE, name), whole)
    driver.spend(1.5 + 1.3e-6 * first[0].size * 4)


def home_lane(driver, name, after=()):
    if after:
        yield Need(*after)
    pairs = yield Need(*[(name, layer, seq) for seq in range(SEQS) for layer in range(2)])
    pairs = [pairs[2 * seq : 2 * seq + 2] for seq in range(SEQS)]
    core, place = lax.axis_index(CORES), lax.axis_index(MP)
    count = lax.axis_size(MP)
    even, half = place % 2 == 0, count // 2
    first_route = [(m, m // 2 if m % 2 == 0 else half + m // 2) for m in range(count)]
    second_route = [(m, half + m // 2 if m % 2 == 0 else m // 2) for m in range(count)]

    def within(route):
        return lambda block: lax.ppermute(block, MP, route)

    def across(route):
        pairs = [(k * count + a, (1 - k) * count + b) for k in range(2) for a, b in route]
        return lambda block: lax.ppermute(block, (CORES, MP), pairs)

    keep = [jnp.where(core == 0, a, b).astype(LOW) for a, b in pairs]
    send = [jnp.where(core == 0, b, a).astype(LOW) for a, b in pairs]
    moves = []
    for kind, rows in ((within, keep), (across, send)):
        moves.append((kind(first_route), jnp.where(even, rows[0], rows[1])))
        moves.append((kind(second_route), jnp.where(even, rows[1], rows[0])))
    driver.spend(4.0)
    got = yield Send(RING, moves, 4 * Z_SLOT, 2.0, 4.0)
    driver.token = got[-1]
    lower = place < half
    kept, other = [
        jnp.concatenate([jnp.where(lower, one, two), jnp.where(lower, two, one)], axis=0)
        for one, two in (got[:2], got[2:])
    ]
    whole = jnp.stack([jnp.where(core == 0, kept, other), jnp.where(core == 0, other, kept)])
    driver.put((HOME, name), whole.astype(F32))
    driver.spend(4.0)


def gain_lane(driver):
    got = yield Need(*[(GAIN, layer, seq) for layer in range(2) for seq in range(SEQS)])
    sums = jnp.stack([got[2 * layer] + got[2 * layer + 1] for layer in range(2)])
    driver.spend(2.0)
    driver.put(GAINS, (yield from summed_everywhere(driver, sums)))


def gather_lane(driver, name, block, after, beside=()):
    if after:
        yield Need(*after)
    (whole,) = yield Send(
        SPARSE, [(lambda x: lax.all_gather(x, MP, axis=0, tiled=True), block)], 46.0
    )
    if beside:
        whole, *_ = lax.optimization_barrier((whole, *beside))
    driver.token = whole
    driver.put(name, whole)


LOGS = []
MATRICES = ((GATE_UP, 9.5), (DOWN, 5.5), (OUT, 3.5), (QKV, 5.0))
WAYS = (
    {GATE_UP: sum_by_both, DOWN: sum_by_both, OUT: sum_by_halving, QKV: sum_by_halving},
    {
        GATE_UP: sum_by_collectives,
        DOWN: sum_by_collectives,
        OUT: sum_by_halving,
        QKV: sum_by_halving,
    },
)
URGENT = 12.0


def shards(
    section_input,
    cotangent,
    pair_owner,
    attn_gain,
    w_query,
    w_key,
    w_value,
    query_gain,
    key_gain,
    w_output,
    mlp_gain,
    w_gate,
    w_up,
    w_down,
):
    n_ctx, n_mp = lax.axis_size(CTX), lax.axis_size(MP)
    core, ctx, place = lax.axis_index(CORES), lax.axis_index(CTX), lax.axis_index(MP)
    is_first = core == 0
    width = section_input.shape[2]
    seq_rows = section_input.shape[1] * n_mp // SEQS
    own_rows = seq_rows // n_mp

    raw_own = lax.dynamic_index_in_dim(section_input, core, 0, keepdims=False)
    top_own = lax.dynamic_index_in_dim(cotangent, core, 0, keepdims=False).astype(LOW)
    ring_order = (place - jnp.arange(n_mp, dtype=jnp.int32)) % n_mp

    def in_ring_order(rows, seq):
        return jnp.concatenate(
            [
                lax.dynamic_slice_in_dim(
                    rows, seq * seq_rows + ring_order[t] * own_rows, own_rows, axis=0
                )
                for t in range(n_mp)
            ],
            axis=0,
        )

    w_qkv = jnp.concatenate([w_query[0], w_key[0], w_value[0]], axis=1)
    own = [w_qkv] + [w[0] for w in (w_output, w_gate, w_up, w_down)]
    other = [swap_cores(w) for w in own]
    own_gains = jnp.concatenate([attn_gain[0], mlp_gain[0], query_gain[0], key_gain[0]])
    other_gains = swap_cores(own_gains)
    gains = []
    for layer in range(2):
        mine = is_first if layer == 0 else ~is_first
        flat = jnp.where(mine, own_gains, other_gains).astype(F32)
        gains.append(
            SimpleNamespace(
                attn=flat[:width],
                mlp=flat[width : 2 * width],
                heads=flat[2 * width :].reshape(2, HD),
            )
        )

    owners = lax.dynamic_index_in_dim(pair_owner, core, 0, keepdims=False)
    index = (ring_order[:, None] * own_rows + jnp.arange(own_rows, dtype=jnp.int32)).reshape(-1)
    inv_freq = ROPE_BASE ** (-jnp.arange(0, HD, 2).astype(F32) / HD)
    seq_tables = []
    for seq in range(SEQS):
        block = jnp.take(owners[seq], ctx ^ jnp.arange(n_ctx, dtype=jnp.int32))[:, None]
        k_pos = jnp.where(
            index < STRETCH,
            block * STRETCH + index,
            (2 * n_ctx - 1 - block) * STRETCH + index - STRETCH,
        )
        q_pos = k_pos[0][:, None]
        angles = q_pos.astype(F32) * inv_freq[None, :]
        cosine, sine = jnp.cos(angles), jnp.sin(angles)
        seq_tables.append(
            (
                jnp.concatenate([cosine, cosine, -sine, sine], axis=1),
                q_pos,
                k_pos,
            )
        )

    q_width, kv_width, ff = w_query.shape[2], w_key.shape[2], w_gate.shape[2]
    widths = {
        QKV: (q_width, kv_width, kv_width),
        OUT: (width,),
        GATE_UP: (ff, ff),
        DOWN: (width,),
    }
    qkv, output, gate, up, down = zip(own, other)
    weights = SimpleNamespace(qkv=qkv, output=output, gate=gate, up=up, down=down)
    driver = Driver(raw_own)
    driver.add(gather_lane(driver, RAW, raw_own, (), other), 0)
    for seq in range(SEQS):
        driver.add(
            sequence_lane(
                driver, seq, weights, gains, seq_tables[seq], own_rows, in_ring_order
            ),
            0,
            seq,
        )
    driver.add(gather_lane(driver, TOP, top_own, (RAW,)), 1)
    for layer in (1, 0):
        for name, cost in MATRICES:
            way = WAYS[layer][name]
            urgent = layer == 0
            lane = matrix_lane(driver, name, layer, cost, way)
            driver.add(lane, 1 if urgent else 3, (name, layer), URGENT if urgent else 3.0)
    for name, _ in MATRICES:
        driver.add(assemble_lane(driver, name, widths[name]), 2)
    driver.add(home_lane(driver, INPUT_GRAD), 1)
    driver.add(home_lane(driver, OUTPUT, ((HOME, INPUT_GRAD),)), 4)
    driver.add(gain_lane(driver), 2)
    driver.run()
    LOGS.append(driver.log)

    def made(key):
        return driver.store[key][1]

    flat = lax.dynamic_index_in_dim(made(GAINS), core, 0, keepdims=False)
    g_query, g_key, g_value = [x[None] for x in made((WHOLE, QKV))]
    g_gate, g_up = [x[None] for x in made((WHOLE, GATE_UP))]
    g_output, g_down = [made((WHOLE, x))[0][None] for x in (OUT, DOWN)]
    return (
        made((HOME, OUTPUT))[None],
        made((HOME, INPUT_GRAD))[None],
        flat[:width][None],
        g_query,
        g_key,
        g_value,
        flat[2 * width : 2 * width + HD][None],
        flat[2 * width + HD :][None],
        g_output,
        flat[width : 2 * width][None],
        g_gate,
        g_up,
        g_down,
    )


def solution(mesh):
    in_specs = (
        P(None, (CTX, MP), None),
        P(None, (CTX, MP), None),
        P(),
        P(CORES, None),
        P(CORES, None, MP),
        P(CORES, None, MP),
        P(CORES, None, MP),
        P(CORES, None),
        P(CORES, None),
        P(CORES, MP, None),
        P(CORES, None),
        P(CORES, None, MP),
        P(CORES, None, MP),
        P(CORES, MP, None),
    )
    out_specs = (
        P(CORES, None, (CTX, MP), None),
        P(CORES, None, (CTX, MP), None),
        P(CORES, None),
        P(CORES, None, MP),
        P(CORES, None, MP),
        P(CORES, None, MP),
        P(CORES, None),
        P(CORES, None),
        P(CORES, MP, None),
        P(CORES, None),
        P(CORES, None, MP),
        P(CORES, None, MP),
        P(CORES, MP, None),
    )
    return jax.shard_map(shards, mesh=mesh, in_specs=in_specs, out_specs=out_specs, check_vma=False)
```

```python
import functools
from types import SimpleNamespace

import jax
import jax.numpy as jnp
from jax import lax
from jax.experimental import pallas as pl
from jax.experimental.pallas import tpu as pltpu
from jax.sharding import PartitionSpec as P

HD = 128
LANES = 128
MB = 2
SEQS = 2
STRETCH = 128
EPSILON = 1e-06
ROPE_BASE = 1000000.0
MASKED_SCORE = -1e30
SCALING = HD ** (-0.5)
LOW = jnp.bfloat16
F32 = jnp.float32
VMEM_SPARE = 12 * 1024 * 1024
VMEM_LEAST = 50 * 1024 * 1024


def dot_nn(left, right):
    return lax.dot_general(left, right, (((1,), (0,)), ((), ())), preferred_element_type=F32)


def dot_nt(left, right):
    return lax.dot_general(left, right, (((1,), (1,)), ((), ())), preferred_element_type=F32)


def dot_tn(left, right):
    return lax.dot_general(left, right, (((0,), (0,)), ((), ())), preferred_element_type=F32)


def kernel_call(body, out_shape, flops, args, layer, weights):
    held = [jax.ShapeDtypeStruct(x.shape, x.dtype) for x in (*args, *[w[0] for w in weights])]
    moved = sum(x.size * x.dtype.itemsize for x in (*held, *out_shape))
    n_args, n_weights, n_out = len(args), len(weights), len(out_shape)

    def whole(*refs):
        ins, rest = refs[:n_args], refs[n_args:]
        pairs, rest = rest[: 2 * n_weights], rest[2 * n_weights :]
        outs, here, sems = rest[:n_out], rest[n_out:-1], rest[-1]
        home = lax.axis_index(CORES) == layer

        def copy(i, source):
            return pltpu.make_async_copy(source, here[i], sems.at[i])

        for i, ref in enumerate(ins):
            copy(i, ref).start()
        for which, taken in ((0, home), (1, jnp.logical_not(home))):

            @pl.when(taken)
            def _(which=which):
                for i in range(n_weights):
                    copy(n_args + i, pairs[2 * i + which]).start()

        def arrived(i):
            copy(n_args + i, pairs[2 * i]).wait()
            return here[n_args + i]

        for i, ref in enumerate(ins):
            copy(i, ref).wait()
        gets = [functools.partial(arrived, i) for i in range(n_weights)]
        body(*here[:n_args], *gets, *outs)

    vmem, hbm = pl.BlockSpec(memory_space=pltpu.VMEM), pl.BlockSpec(memory_space=pltpu.HBM)
    return pl.pallas_call(
        whole,
        out_shape=out_shape,
        in_specs=[hbm] * (n_args + 2 * n_weights),
        out_specs=[vmem] * n_out,
        scratch_shapes=[pltpu.VMEM(x.shape, x.dtype) for x in held]
        + [pltpu.SemaphoreType.DMA((len(held),))],
        compiler_params=pltpu.CompilerParams(vmem_limit_bytes=max(moved + VMEM_SPARE, VMEM_LEAST)),
        cost_estimate=pl.CostEstimate(flops=flops, bytes_accessed=moved, transcendentals=0),
    )(*args, *[ref for w in weights for ref in w])


def qkv_forward_body(q_width, x, gains, turns, get_qkv, proj, queries, kv):
    cos_full, sin_signed = turns[:, :HD], turns[:, HD:]

    def prepared(head, gain):
        scaling = lax.rsqrt(jnp.mean(head * head, axis=-1, keepdims=True) + EPSILON)
        normed = head * scaling * gain
        return (normed * cos_full + pltpu.roll(normed, HD // 2, 1) * sin_signed).astype(LOW)

    mixed = dot_nn(x[...], get_qkv()[...])
    both = proj.shape[1]
    proj[...] = mixed[:, :both]
    for at in range(0, q_width, HD):
        queries[:, at : at + HD] = prepared(mixed[:, at : at + HD], gains[:1, :])
    for at in range(q_width, both, HD):
        kv[:, at - q_width : at - q_width + HD] = prepared(mixed[:, at : at + HD], gains[1:, :])
    kv[:, both - q_width :] = mixed[:, both:].astype(LOW)


def mlp_forward_body(x, get_gate, get_up, get_down, gate, up, hidden, *parts):
    rows = x[...]
    gate_all = dot_nn(rows, get_gate()[...])
    up_all = dot_nn(rows, get_up()[...])
    gate[...] = gate_all.astype(LOW)
    up[...] = up_all.astype(LOW)
    hidden[...] = (jax.nn.silu(gate_all) * up_all).astype(LOW)
    store_product(parts, hidden[...], get_down(), dot_nn)


def mlp_back_body(branch, gate, up, get_down, get_gate, get_up, grad_gate, grad_up, *parts):
    grad_hidden = dot_nt(branch[...], get_down()[...])
    gate_all, up_all = gate[...].astype(F32), up[...].astype(F32)
    sig = jax.nn.sigmoid(gate_all)
    grad_gate[...] = (grad_hidden * up_all * sig * (1.0 + gate_all * (1.0 - sig))).astype(LOW)
    grad_up[...] = (grad_hidden * gate_all * sig).astype(LOW)
    w_gate, w_up = get_gate(), get_up()
    for at in range(0, w_gate.shape[0], 512):
        here = pl.ds(at, 512)
        total = dot_nt(grad_gate[...], w_gate[here, :]) + dot_nt(grad_up[...], w_up[here, :])
        store_columns(parts, here, total)


def store_columns(parts, here, rows):
    size = parts[0].shape[0]
    for i, part in enumerate(parts):
        part[:, here] = rows[i * size : (i + 1) * size].astype(LOW)


def store_product(parts, rows, weight, dot):
    for at in range(0, weight.shape[1], 512):
        here = pl.ds(at, 512)
        store_columns(parts, here, dot(rows, weight[:, here]))


def store_blocks(parts, rows):
    size = parts[0].shape[0]
    for i, part in enumerate(parts):
        part[...] = rows[i * size : (i + 1) * size].astype(LOW)


def attend_body(n_ctx, queries, *refs):
    blocks = refs[:n_ctx]
    q_pos, k_pos, get_out = refs[n_ctx : n_ctx + 3]
    attended, log_total, *parts = refs[n_ctx + 3 :]
    rows = queries.shape[0]
    kv_width = blocks[0].shape[1] // 2
    groups = queries.shape[1] // kv_width
    place = jnp.concatenate([q_pos[...]] * groups, axis=0)
    for kv_head in range(kv_width // HD):
        first = kv_head * groups
        stacked = jnp.concatenate(
            [queries[:, (first + i) * HD : (first + i + 1) * HD] for i in range(groups)], axis=0
        )
        at = kv_head * HD
        scores = []
        for j, block in enumerate(blocks):
            raw = dot_nt(stacked, block[:, at : at + HD]) * SCALING
            scores.append(jnp.where(k_pos[j : j + 1, :] <= place, raw, MASKED_SCORE))
        top = functools.reduce(
            jnp.maximum, [jnp.max(s, axis=1, keepdims=True) for s in scores]
        )
        total, running = 0.0, 0.0
        for s, block in zip(scores, blocks):
            weights = jnp.exp(s - top)
            total = total + jnp.sum(weights, axis=1, keepdims=True)
            running = running + dot_nn(
                weights.astype(LOW), block[:, kv_width + at : kv_width + at + HD]
            )
        result = (running / total).astype(LOW)
        logs = top + jnp.log(total)
        for i in range(groups):
            head = first + i
            attended[:, head * HD : (head + 1) * HD] = result[i * rows : (i + 1) * rows]
            log_total[:, head : head + 1] = logs[i * rows : (i + 1) * rows]
    store_blocks(parts, dot_nn(attended[...], get_out()[...]))


def attend_back_body(n_ctx, grad_rows, queries, *refs):
    blocks = refs[:n_ctx]
    q_pos, k_pos, attended, log_total, get_out, grad_q = refs[n_ctx : n_ctx + 6]
    grad_kv = refs[n_ctx + 6 :]
    rows = queries.shape[0]
    kv_width = blocks[0].shape[1] // 2
    groups = queries.shape[1] // kv_width
    grad_all = dot_nt(grad_rows[...], get_out()[...]).astype(LOW)
    place = jnp.concatenate([q_pos[...]] * groups, axis=0)
    for kv_head in range(kv_width // HD):
        heads = [kv_head * groups + i for i in range(groups)]
        stacked = jnp.concatenate([queries[:, h * HD : (h + 1) * HD] for h in heads], axis=0)
        grads = jnp.concatenate([grad_all[:, h * HD : (h + 1) * HD] for h in heads], axis=0)
        out_low = jnp.concatenate([attended[:, h * HD : (h + 1) * HD] for h in heads], axis=0)
        logs = jnp.concatenate([log_total[:, h : h + 1] for h in heads], axis=0)
        delta = jnp.sum(grads.astype(F32) * out_low.astype(F32), axis=1, keepdims=True)
        at = kv_head * HD
        total = 0.0
        for j, block in enumerate(blocks):
            keys = block[:, at : at + HD]
            values = block[:, kv_width + at : kv_width + at + HD]
            shifted = dot_nt(stacked, keys) * SCALING - logs
            probs = jnp.exp(jnp.where(k_pos[j : j + 1, :] <= place, shifted, MASKED_SCORE))
            grad_scores = (probs * (dot_nt(grads, values) - delta)).astype(LOW)
            total = total + dot_nn(grad_scores, keys)
            grad_kv[j][:, at : at + HD] = (dot_tn(grad_scores, stacked) * SCALING).astype(LOW)
            grad_kv[j][:, kv_width + at : kv_width + at + HD] = dot_tn(
                probs.astype(LOW), grads
            ).astype(LOW)
        for i, h in enumerate(heads):
            grad_q[:, h * HD : (h + 1) * HD] = total[i * rows : (i + 1) * rows] * SCALING


def qkv_back_body(n_ctx, grad_q, *refs):
    grad_kv = refs[:n_ctx]
    proj, gains, turns, get_qkv, mixed, grad_gains, *parts = refs[n_ctx:]
    cos_full, sin_signed = turns[:, :HD], turns[:, HD:]
    q_width = grad_q.shape[1]
    kv_width = proj.shape[1] - q_width

    def pulled(grad, head, gain):
        turned = grad * cos_full + pltpu.roll(grad * sin_signed, HD // 2, 1)
        scaling = lax.rsqrt(jnp.mean(head * head, axis=-1, keepdims=True) + EPSILON)
        inner = turned * gain
        back = scaling * inner - head * (
            scaling * scaling * scaling * jnp.mean(inner * head, axis=-1, keepdims=True)
        )
        return back.astype(LOW), jnp.sum(turned * head * scaling, axis=0, keepdims=True)

    total = 0.0
    for at in range(0, q_width, HD):
        back, gain_part = pulled(grad_q[:, at : at + HD], proj[:, at : at + HD], gains[:1, :])
        mixed[:, at : at + HD] = back
        total = total + gain_part
    grad_gains[:1, :] = total
    summed = functools.reduce(jnp.add, [g[...].astype(F32) for g in grad_kv])
    total = 0.0
    for at in range(0, kv_width, HD):
        here = slice(q_width + at, q_width + at + HD)
        back, gain_part = pulled(summed[:, at : at + HD], proj[:, here], gains[1:, :])
        mixed[:, here] = back
        total = total + gain_part
    grad_gains[1:, :] = total
    mixed[:, q_width + kv_width :] = summed[:, kv_width:].astype(LOW)
    w_qkv = get_qkv()
    for at in range(0, w_qkv.shape[0], 512):
        here = pl.ds(at, 512)
        store_columns(parts, here, dot_nt(mixed[...], w_qkv[here, :]))


def product_body(n_left, n_right, place, *refs):
    lefts, refs = refs[:n_left], refs[n_left:]
    groups = []
    for count in n_right:
        groups.append(refs[:count])
        refs = refs[count:]
    *extra, out, left_all, right_all, sems = refs
    tile, rows = out.shape[0], left_all.shape[1]
    step = pl.program_id(0)

    @pl.when(step == 0)
    def _():
        copies = []
        row = 0
        for ref in lefts:
            source = ref.at[:, pl.ds(pl.multiple_of(place[0] * rows, rows), rows)]
            copies.append((source, left_all.at[pl.ds(row, ref.shape[0]), :]))
            row += ref.shape[0]
        column = 0
        for group in groups:
            row = 0
            for ref in group:
                here = (pl.ds(row, ref.shape[0]), pl.ds(column, ref.shape[1]))
                copies.append((ref, right_all.at[here]))
                row += ref.shape[0]
            column += group[0].shape[1]
        copies = [
            pltpu.make_async_copy(source, target, sems.at[i])
            for i, (source, target) in enumerate(copies)
        ]
        for copy in copies:
            copy.start()
        for copy in copies:
            copy.wait()

    left = left_all[:, pl.ds(pl.multiple_of(step * tile, tile), tile)]
    width = 512
    for at in range(0, out.shape[1], width):
        result = dot_tn(left, right_all[:, at : at + width])
        if extra:
            result = result + extra[0][:, at : at + width].astype(F32)
        out[:, at : at + width] = result.astype(LOW)


def piece_product(pieces, which, lefts, rights, extra=None, extra_at=0):
    depth = sum(x.shape[0] for x in lefts)
    rows = lefts[0].shape[1] // pieces
    cols = sum(group[0].shape[1] for group in rights)
    tile = 256
    while rows % tile:
        tile //= 2
    steps = rows // tile
    flat = [x for group in rights for x in group]
    extras = [] if extra is None else [extra]
    place = jnp.stack([jnp.asarray(which, jnp.int32), jnp.asarray(extra_at, jnp.int32)])
    held = 2 * depth * (rows + cols)
    return pl.pallas_call(
        functools.partial(product_body, len(lefts), [len(group) for group in rights]),
        out_shape=jax.ShapeDtypeStruct((rows, cols), LOW),
        grid_spec=pltpu.PrefetchScalarGridSpec(
            num_scalar_prefetch=1,
            grid=(steps,),
            in_specs=[pl.BlockSpec(memory_space=pltpu.HBM)] * (len(lefts) + len(flat))
            + [
                pl.BlockSpec((tile, cols), lambda i, place: (place[1] * steps + i, 0))
                for _ in extras
            ],
            out_specs=pl.BlockSpec((tile, cols), lambda i, place: (i, 0)),
            scratch_shapes=[
                pltpu.VMEM((depth, rows), LOW),
                pltpu.VMEM((depth, cols), LOW),
                pltpu.SemaphoreType.DMA((len(lefts) + len(flat),)),
            ],
        ),
        compiler_params=pltpu.CompilerParams(
            vmem_limit_bytes=max(held + 8 * tile * cols + VMEM_SPARE, VMEM_LEAST)
        ),
        cost_estimate=pl.CostEstimate(
            flops=2 * depth * rows * cols,
            bytes_accessed=held + 2 * rows * cols * (1 + len(extras)),
            transcendentals=0,
        ),
    )(place, *lefts, *flat, *extras)


def assemble_body(widths, place, *refs):
    ins, outs = refs[:4], refs[4:]
    step = pl.program_id(0)
    for i in range(4):

        @pl.when((step == i % 2) & (place[0] == i // 2))
        def _(i=i):
            at = 0
            for out, width in zip(outs, widths):
                out[...] = ins[i][:, at : at + width].astype(F32)
                at += width


def assemble(place, arrays, widths):
    rows, cols = arrays[0].shape
    tile = 256
    while rows % tile:
        tile //= 2
    steps = rows // tile

    def in_map(i, step, t, place):
        wanted = place[0] == i // 2
        if i % 2 == 0:
            moving = jnp.where(step == 0, t, steps - 1)
        else:
            moving = jnp.where(step == 0, 0, t)
        return (jnp.where(wanted, moving, 0), 0)

    def out_map(step, t, place):
        return ((place[0] ^ step) * steps + t, 0)

    return pl.pallas_call(
        functools.partial(assemble_body, widths),
        out_shape=[jax.ShapeDtypeStruct((2 * rows, w), F32) for w in widths],
        grid_spec=pltpu.PrefetchScalarGridSpec(
            num_scalar_prefetch=1,
            grid=(2, steps),
            in_specs=[pl.BlockSpec((tile, cols), functools.partial(in_map, i)) for i in range(4)],
            out_specs=[pl.BlockSpec((tile, w), out_map) for w in widths],
        ),
        compiler_params=pltpu.CompilerParams(vmem_limit_bytes=24 * tile * cols + VMEM_SPARE),
        cost_estimate=pl.CostEstimate(
            flops=0, bytes_accessed=2 * rows * cols * 6, transcendentals=0
        ),
    )(place, *arrays)


Z_SLOT, Z_HOP = 5.5, 3.2


START_COST = 0.9
AHEAD = 10.0
RING, LINKS, SWAP, SPARSE, NONE = range(5)
RAW, TOP, OUTPUT, INPUT_GRAD, GAIN, GAINS, HALF, WHOLE, HOME, GATE_UP, DOWN, OUT, QKV = range(13)
CORES, CTX, MP = "section", "ctx", "mp"


class Send:
    def __init__(self, kind, blocks, span, then=0.0, slack=0.0):
        self.kind, self.blocks, self.span, self.then, self.slack = kind, blocks, span, then, slack


class Need:
    def __init__(self, *keys, then=0.0):
        self.keys, self.then = keys, then


class Wait:
    def __init__(self, until):
        self.until = until


class Lane:
    def __init__(self, work, rank, name, patience):
        self.work, self.rank, self.name, self.patience = work, rank, name, patience
        self.ready, self.value, self.wanted, self.then = 0.0, None, None, 0.0


class Driver:
    def __init__(self, token):
        self.token, self.now, self.cost = token, 0.0, 0.0
        self.lanes, self.store, self.log = [], {}, []
        self.free = [0.0] * 5

    def spend(self, cost):
        self.cost += cost

    def put(self, key, value):
        self.store[key] = (self.now + self.cost, value)

    def add(self, work, rank, name=None, patience=3.0):
        lane = Lane(work, rank, name, patience)
        lane.ready = self.now
        self.lanes.append(lane)

    def tied(self, value):
        leaves, tree = jax.tree.flatten(value)
        if not leaves:
            return value
        *leaves, _ = lax.optimization_barrier((*leaves, self.token))
        return jax.tree.unflatten(tree, leaves)

    def turn(self):
        while self.free[LINKS] > self.now + AHEAD:
            yield Wait(self.free[LINKS] - AHEAD)

    def ready_at(self, lane):
        if lane.wanted is None:
            return lane.ready
        if any(key not in self.store for key in lane.wanted):
            return None
        return max([lane.ready] + [self.store[key][0] for key in lane.wanted])

    def step(self, lane):
        self.log.append((self.now, self.ready_at(lane), lane.name))
        self.now = max(self.now, self.ready_at(lane))
        if lane.wanted is not None:
            lane.value = tuple(self.store[key][1] for key in lane.wanted)
            lane.wanted = None
        self.cost = 0.0
        value = None if lane.value is None else self.tied(lane.value)
        lane.value = None
        try:
            request = lane.work.send(value)
        except StopIteration:
            self.lanes.remove(lane)
            self.now += self.cost
            return
        self.now += self.cost
        if isinstance(request, Wait):
            lane.ready = max(self.now, request.until)
            return
        lane.then = request.then
        if isinstance(request, Need):
            lane.wanted, lane.ready = request.keys, self.now
            return
        self.now += START_COST * len(request.blocks)
        start = max(self.now, self.free[request.kind])
        self.free[request.kind] = start + request.span
        lane.ready = start + request.span + Z_HOP + request.slack
        lane.value = [move(block) for move, block in request.blocks]
        self.token = request.blocks[0][1]

    def run(self):
        while self.lanes:
            times = [(self.ready_at(lane), lane) for lane in self.lanes]
            times = [(at, lane) for at, lane in times if at is not None]
            main = [pair for pair in times if pair[1].rank == 0]
            soon = min([at for at, _ in main], default=1e9)
            waiting = [
                (at, lane)
                for at, lane in times
                if at <= self.now
                and (lane.rank == 0 or max(self.now, at) + lane.then <= soon + lane.patience)
            ]
            if waiting:
                lane = min(waiting, key=lambda pair: (pair[1].rank, pair[0]))[1]
            elif main:
                lane = min(
                    [p for p in times if p[1].rank == 0 or p[0] + p[1].then <= soon + p[1].patience],
                    key=lambda pair: (pair[0], pair[1].rank),
                )[1]
            else:
                lane = min(times, key=lambda pair: (pair[0], pair[1].rank))[1]
            self.step(lane)


def swap_cores(block):
    return lax.ppermute(block, CORES, [(0, 1), (1, 0)])


def to_core(core):
    return lambda block: lax.ppermute(block, CORES, [(1 - core, core)])


def ring_step(block):
    count = lax.axis_size(MP)
    return lax.ppermute(block, MP, [(i, (i + 1) % count) for i in range(count)])


def across_ctx(distance):
    count = lax.axis_size(CTX)
    return lambda block: lax.ppermute(block, CTX, [(i, i ^ distance) for i in range(count)])


def ring_gather(driver, block):
    blocks = [block]
    for _ in range(lax.axis_size(MP) - 1):
        (block,) = yield Send(RING, [(ring_step, block)], Z_SLOT)
        blocks.append(block)
    driver.spend(1.5)
    return lax.optimization_barrier(jnp.concatenate(blocks, axis=0))


def ring_sum(driver, part):
    count = lax.axis_size(MP)
    if not isinstance(part, list):
        rows = part.shape[0] // count
        part = [part[t * rows : (t + 1) * rows] for t in range(count)]
        driver.spend(0.8)
    running = part[1]
    for t in range(2, count):
        (got,) = yield Send(RING, [(ring_step, running)], Z_SLOT)
        running = (got.astype(F32) + part[t].astype(F32)).astype(LOW)
        driver.spend(1.4)
    (got,) = yield Send(RING, [(ring_step, running)], Z_SLOT)
    driver.spend(1.4)
    return got.astype(F32) + part[0].astype(F32)


def ctx_exchange(blocks, span=12.0):
    moves = [(across_ctx(j + 1), block) for j, block in enumerate(blocks)]
    got = yield Send(LINKS, moves, span)
    return got


def summed_everywhere(driver, block):
    for axis in (MP, CORES, CTX):
        count = lax.axis_size(axis)
        distance = 1
        while distance < count:
            route = [(i, i ^ distance) for i in range(count)]
            (got,) = yield Send(
                LINKS if axis == CTX else NONE,
                [(functools.partial(lax.ppermute, axis_name=axis, perm=route), block)],
                2.0,
                1.0,
                5.0,
            )
            block = block + got
            driver.spend(1.0)
            distance *= 2
    return block


def row_norm(rows, gain):
    scaling = lax.rsqrt(jnp.mean(rows * rows, axis=-1, keepdims=True) + EPSILON)
    return rows * scaling * gain


def row_norm_back(rows, gain, grad):
    scaling = lax.rsqrt(jnp.mean(rows * rows, axis=-1, keepdims=True) + EPSILON)
    inner = grad * gain
    back = scaling * inner - rows * (
        scaling * scaling * scaling * jnp.mean(inner * rows, axis=-1, keepdims=True)
    )
    return back, jnp.sum(grad * rows * scaling, axis=0)


def shape(rows, cols, kind=LOW):
    return jax.ShapeDtypeStruct((rows, cols), kind)


def part_shapes(rows, width):
    count = lax.axis_size(MP)
    return [shape(rows // count, width)] * count


def project(attn_in, layer, weights, gains, tables):
    turns, q_pos, k_pos = tables
    rows, width = attn_in.shape
    total = weights.qkv[0].shape[1]
    q_width = weights.output[0].shape[0]
    kv_width = (total - q_width) // 2
    return kernel_call(
        functools.partial(qkv_forward_body, q_width),
        [shape(rows, q_width + kv_width, F32), shape(rows, q_width), shape(rows, 2 * kv_width)],
        2 * rows * width * total,
        (attn_in, gains.heads, turns),
        layer,
        [weights.qkv],
    )


def attend(queries, blocks, layer, weights, tables):
    turns, q_pos, k_pos = tables
    rows, q_width = queries.shape
    width = weights.output[0].shape[1]
    attended, log_total, *parts = kernel_call(
        functools.partial(attend_body, len(blocks)),
        [shape(rows, q_width), shape(rows, q_width // HD, F32)] + part_shapes(rows, width),
        2 * rows * q_width * (2 * rows * len(blocks) + width),
        (queries, *blocks, q_pos, k_pos),
        layer,
        [weights.output],
    )
    return parts, attended, log_total


def mlp_forward(mlp_in, layer, weights):
    ff = weights.gate[0].shape[1]
    picked = [weights.gate, weights.up, weights.down]
    rows, width = mlp_in.shape
    gate, up, hidden, *parts = kernel_call(
        mlp_forward_body,
        [shape(rows, ff)] * 3 + part_shapes(rows, width),
        6 * rows * width * ff,
        (mlp_in,),
        layer,
        picked,
    )
    return gate, up, hidden, parts


def mlp_back(branch, kept, layer, weights):
    ff = weights.gate[0].shape[1]
    picked = [weights.down, weights.gate, weights.up]
    rows, width = branch.shape
    grad_gate, grad_up, *parts = kernel_call(
        mlp_back_body,
        [shape(rows, ff)] * 2 + part_shapes(rows, width),
        6 * rows * width * ff,
        (branch, kept.gate, kept.up),
        layer,
        picked,
    )
    return grad_gate, grad_up, parts


def attend_back(grad_rows, kept, layer, weights, tables):
    turns, q_pos, k_pos = tables
    blocks = kept.blocks
    rows, q_width = kept.queries.shape
    return kernel_call(
        functools.partial(attend_back_body, len(blocks)),
        [shape(rows, q_width, F32)] + [shape(*blocks[0].shape)] * len(blocks),
        2 * rows * q_width * (5 * rows * len(blocks) + grad_rows.shape[1]),
        (
            grad_rows,
            kept.queries,
            *blocks,
            q_pos,
            k_pos,
            kept.attended,
            kept.log_total,
        ),
        layer,
        [weights.output],
    )


def project_back(grad_q, grad_kv, kept, layer, weights, gains, tables):
    turns, q_pos, k_pos = tables
    rows, width = kept.attn_in.shape
    total = weights.qkv[0].shape[1]
    mixed, grad_gains, *parts = kernel_call(
        functools.partial(qkv_back_body, len(grad_kv)),
        [shape(rows, total), shape(2, HD, F32)] + part_shapes(rows, width),
        2 * rows * width * total,
        (grad_q, *grad_kv, kept.proj, gains.heads, turns),
        layer,
        [weights.qkv],
    )
    return mixed, parts, grad_gains


def sequence_lane(driver, seq, weights, gains, tables, own_rows, in_ring_order):
    (raw,) = yield Need(RAW)
    rows = in_ring_order(raw, seq)
    h_rows = rows[:own_rows].astype(F32)
    kept = []
    for layer in range(2):
        gain = gains[layer]
        if layer == 0:
            attn_in = row_norm(rows.astype(F32), gain.attn).astype(LOW)
            driver.spend(4.0)
        else:
            attn_in = yield from ring_gather(driver, row_norm(h_rows, gain.attn).astype(LOW))
        proj, queries, kv = project(attn_in, layer, weights, gain, tables)
        driver.spend(6.0)
        others = yield from ctx_exchange([kv] * (lax.axis_size(CTX) - 1))
        blocks = [kv] + others
        part, attended, log_total = attend(queries, blocks, layer, weights, tables)
        driver.spend(6.0)
        mid = h_rows + (yield from ring_sum(driver, part))
        driver.spend(1.0)
        mlp_in = yield from ring_gather(driver, row_norm(mid, gain.mlp).astype(LOW))
        gate, up, hidden, part = mlp_forward(mlp_in, layer, weights)
        driver.spend(9.5)
        kept.append(
            SimpleNamespace(
                attn_in=attn_in,
                h_rows=h_rows,
                proj=proj,
                queries=queries,
                blocks=blocks,
                attended=attended,
                log_total=log_total,
                mid=mid,
                mlp_in=mlp_in,
                gate=gate,
                up=up,
                hidden=hidden,
            )
        )
        h_rows = mid + (yield from ring_sum(driver, part))
        driver.spend(1.0)
        driver.put((OUTPUT, layer, seq), h_rows)

    (top_grad,) = yield Need(TOP)
    branch = in_ring_order(top_grad, seq)
    driver.spend(2.0)
    grad_out = branch[:own_rows].astype(F32)
    for layer in (1, 0):
        gain, state = gains[layer], kept[layer]
        if layer == 0:
            branch = yield from ring_gather(driver, grad_out.astype(LOW))
        driver.put((DOWN, layer, seq), (state.hidden, branch))
        grad_gate, grad_up, part = mlp_back(branch, state, layer, weights)
        driver.spend(12.0)
        driver.put((GATE_UP, layer, seq), (state.mlp_in, grad_gate, grad_up))
        back, mlp_gain = row_norm_back(
            state.mid, gain.mlp, (yield from ring_sum(driver, part))
        )
        driver.spend(4.0)
        grad_mid = grad_out + back
        grad_rows = yield from ring_gather(driver, grad_mid.astype(LOW))
        driver.put((OUT, layer, seq), (state.attended, grad_rows))
        grad_q, *grad_kv = attend_back(grad_rows, state, layer, weights, tables)
        driver.spend(10.0)
        grad_kv = [grad_kv[0]] + (yield from ctx_exchange(grad_kv[1:], 17.0))
        mixed, part, head_gains = project_back(
            grad_q, grad_kv, state, layer, weights, gain, tables
        )
        driver.spend(9.0)
        driver.put((QKV, layer, seq), (state.attn_in, mixed))
        back, attn_gain = row_norm_back(
            state.h_rows, gain.attn, (yield from ring_sum(driver, part))
        )
        driver.spend(4.0)
        grad_out = grad_mid + back
        driver.put((INPUT_GRAD, layer, seq), grad_out)
        driver.put(
            (GAIN, layer, seq), jnp.concatenate([attn_gain, mlp_gain, head_gains.reshape(-1)])
        )


def core_bit(t, bits):
    shift = jnp.where(lax.axis_index(CORES) == 0, t, bits - 1 - t)
    return (lax.axis_index(CTX) >> shift) & 1


def joint_step(t, bits):
    count = 1 << bits
    route = []
    for core in range(2):
        distance = 1 << (t if core == 0 else bits - 1 - t)
        route += [(core * count + i, core * count + (i ^ distance)) for i in range(count)]
    return lambda block: lax.ppermute(block, (CORES, CTX), route)


def sum_by_halving(driver, product, rows, cost, slack):
    core = lax.axis_index(CORES)
    bits = lax.axis_size(CTX).bit_length() - 1
    flag = core_bit(0, bits)
    sent = None
    if rows % (4 * LANES) == 0:
        sent = product(4, 2 * core + 1 - flag, 1 - flag)
        total = product(4, 2 * core + flag, flag)
    else:
        total = product(2, core, 0)
    driver.spend(cost * 1.4)
    for t in range(bits):
        if sent is None:
            flag, count = core_bit(t, bits), total.shape[0] // 2
            sent = lax.dynamic_slice_in_dim(total, (1 - flag) * count, count, axis=0)
            total = lax.dynamic_slice_in_dim(total, flag * count, count, axis=0)
            driver.spend(1.5 + sent.size * 2 / 1e6)
        size = sent.size * 2 / 1e6
        (got,) = yield Send(
            LINKS, [(joint_step(t, bits), sent)], 11.5 * size, 1.5 + size, slack + 6.0 * size
        )
        driver.spend(1.0 + size)
        total = (total.astype(F32) + got.astype(F32)).astype(LOW)
        sent = None
    for t in reversed(range(bits)):
        size = total.size * 2 / 1e6
        (got,) = yield Send(
            LINKS, [(joint_step(t, bits), total)], 11.5 * size, 1.5 + 2 * size, slack + 6.0 * size
        )
        flag = core_bit(t, bits) == 0
        total = jnp.concatenate(
            [jnp.where(flag, total, got), jnp.where(flag, got, total)], axis=0
        )
        driver.spend(1.5 + 2 * size)
    return total


def scattered(driver, product, cost, crowding):
    total = product(2, lax.axis_index(CORES), 0)
    driver.spend(cost * 1.2)
    move = functools.partial(lax.psum_scatter, axis_name=CTX, scatter_dimension=0, tiled=True)
    span = (13 + 2e-5 * total.size) * crowding
    (share,) = yield Send(SPARSE, [(move, total)], span, 1.0)
    return share, span


def sum_by_collectives(driver, product, rows, cost, slack):
    share, span = yield from scattered(driver, product, cost, 1.0)
    move = functools.partial(lax.all_gather, axis_name=CTX, axis=0, tiled=True)
    (total,) = yield Send(SPARSE, [(move, share)], span, 1.0)
    return total


def sum_by_both(driver, product, rows, cost, slack):
    if lax.axis_size(CTX) != 4:
        return (yield from sum_by_collectives(driver, product, rows, cost, slack))
    share, _ = yield from scattered(driver, product, cost, 1.35)
    first = lax.axis_index(CORES) == 0
    size = share.size * 2 / 1e6
    (got,) = yield Send(
        LINKS, [(joint_step(0, 2), share)], 11.5 * size, 1.5 + 2 * size, slack + 3.0 * size
    )
    flag = core_bit(0, 2) == 0
    pair = jnp.stack([jnp.where(flag, share, got), jnp.where(flag, got, share)])
    driver.spend(1.5 + 2 * size)
    (got,) = yield Send(
        LINKS, [(joint_step(1, 2), pair)], 23.0 * size, 2.0 + 4 * size, slack + 6.0 * size
    )
    flag = core_bit(1, 2) == 0
    low, high = jnp.where(flag, pair, got), jnp.where(flag, got, pair)
    driver.spend(2.0 + 4 * size)
    return jnp.concatenate(
        [
            low[0],
            jnp.where(first, low[1], high[0]),
            jnp.where(first, high[0], low[1]),
            high[1],
        ],
        axis=0,
    )


def matrix_lane(driver, name, layer, cost, way):
    parts = yield Need(*[(name, layer, seq) for seq in range(SEQS)], then=cost)
    lefts = [part[0] for part in parts]
    rights = [[part[at] for part in parts] for at in range(1, len(parts[0]))]
    driver.spend(cost)
    away = piece_product(2, 1 - lax.axis_index(CORES), lefts, rights)
    size = away.size * 2 / 1e6
    (received,) = yield Send(SWAP, [(swap_cores, away)], 2.0 + 1.6 * size, cost * 1.3, 4.0)

    def product(pieces, which, extra_at):
        return piece_product(pieces, which, lefts, rights, received, extra_at)

    slack = 4.0 if layer == 0 else 25.0
    half = yield from way(driver, product, lefts[0].shape[1], cost, slack)
    (other,) = yield Send(SWAP, [(to_core(layer), half)], 2.0 + 1.6 * size, 0.0, 4.0)
    driver.token = other
    driver.put((HALF, name, layer), (half, other))


def assemble_lane(driver, name, widths):
    first, second = yield Need((HALF, name, 0), (HALF, name, 1))
    core = lax.axis_index(CORES).astype(jnp.int32).reshape(1)
    whole = assemble(core, [*first, *second], widths)
    driver.token = whole[0]
    driver.put((WHOLE, name), whole)
    driver.spend(1.5 + 1.3e-6 * first[0].size * 4)


def home_lane(driver, name, after=()):
    if after:
        yield Need(*after)
    pairs = yield Need(*[(name, layer, seq) for seq in range(SEQS) for layer in range(2)])
    pairs = [pairs[2 * seq : 2 * seq + 2] for seq in range(SEQS)]
    core, place = lax.axis_index(CORES), lax.axis_index(MP)
    count = lax.axis_size(MP)
    even, half = place % 2 == 0, count // 2
    first_route = [(m, m // 2 if m % 2 == 0 else half + m // 2) for m in range(count)]
    second_route = [(m, half + m // 2 if m % 2 == 0 else m // 2) for m in range(count)]

    def within(route):
        return lambda block: lax.ppermute(block, MP, route)

    def across(route):
        pairs = [(k * count + a, (1 - k) * count + b) for k in range(2) for a, b in route]
        return lambda block: lax.ppermute(block, (CORES, MP), pairs)

    keep = [jnp.where(core == 0, a, b).astype(LOW) for a, b in pairs]
    send = [jnp.where(core == 0, b, a).astype(LOW) for a, b in pairs]
    moves = []
    for kind, rows in ((within, keep), (across, send)):
        moves.append((kind(first_route), jnp.where(even, rows[0], rows[1])))
        moves.append((kind(second_route), jnp.where(even, rows[1], rows[0])))
    driver.spend(4.0)
    got = yield Send(RING, moves, 4 * Z_SLOT, 2.0, 4.0)
    driver.token = got[-1]
    lower = place < half
    kept, other = [
        jnp.concatenate([jnp.where(lower, one, two), jnp.where(lower, two, one)], axis=0)
        for one, two in (got[:2], got[2:])
    ]
    whole = jnp.stack([jnp.where(core == 0, kept, other), jnp.where(core == 0, other, kept)])
    driver.put((HOME, name), whole.astype(F32))
    driver.spend(4.0)


def gain_lane(driver):
    got = yield Need(*[(GAIN, layer, seq) for layer in range(2) for seq in range(SEQS)])
    sums = jnp.stack([got[2 * layer] + got[2 * layer + 1] for layer in range(2)])
    driver.spend(2.0)
    driver.put(GAINS, (yield from summed_everywhere(driver, sums)))


def gather_lane(driver, name, block, after, beside=()):
    if after:
        yield Need(*after)
    (whole,) = yield Send(
        SPARSE, [(lambda x: lax.all_gather(x, MP, axis=0, tiled=True), block)], 46.0
    )
    if beside:
        whole, *_ = lax.optimization_barrier((whole, *beside))
    driver.token = whole
    driver.put(name, whole)


LOGS = []
MATRICES = ((GATE_UP, 9.5), (DOWN, 5.5), (OUT, 3.5), (QKV, 5.0))
WAYS = (
    {GATE_UP: sum_by_both, DOWN: sum_by_both, OUT: sum_by_halving, QKV: sum_by_halving},
    {
        GATE_UP: sum_by_collectives,
        DOWN: sum_by_collectives,
        OUT: sum_by_halving,
        QKV: sum_by_halving,
    },
)
URGENT = 12.0


def shards(
    section_input,
    cotangent,
    pair_owner,
    attn_gain,
    w_query,
    w_key,
    w_value,
    query_gain,
    key_gain,
    w_output,
    mlp_gain,
    w_gate,
    w_up,
    w_down,
):
    n_ctx, n_mp = lax.axis_size(CTX), lax.axis_size(MP)
    core, ctx, place = lax.axis_index(CORES), lax.axis_index(CTX), lax.axis_index(MP)
    is_first = core == 0
    width = section_input.shape[2]
    seq_rows = section_input.shape[1] * n_mp // SEQS
    own_rows = seq_rows // n_mp

    raw_own = lax.dynamic_index_in_dim(section_input, core, 0, keepdims=False)
    top_own = lax.dynamic_index_in_dim(cotangent, core, 0, keepdims=False).astype(LOW)
    ring_order = (place - jnp.arange(n_mp, dtype=jnp.int32)) % n_mp

    def in_ring_order(rows, seq):
        return jnp.concatenate(
            [
                lax.dynamic_slice_in_dim(
                    rows, seq * seq_rows + ring_order[t] * own_rows, own_rows, axis=0
                )
                for t in range(n_mp)
            ],
            axis=0,
        )

    w_qkv = jnp.concatenate([w_query[0], w_key[0], w_value[0]], axis=1)
    own = [w_qkv] + [w[0] for w in (w_output, w_gate, w_up, w_down)]
    other = [swap_cores(w) for w in own]
    own_gains = jnp.concatenate([attn_gain[0], mlp_gain[0], query_gain[0], key_gain[0]])
    other_gains = swap_cores(own_gains)
    gains = []
    for layer in range(2):
        mine = is_first if layer == 0 else ~is_first
        flat = jnp.where(mine, own_gains, other_gains).astype(F32)
        gains.append(
            SimpleNamespace(
                attn=flat[:width],
                mlp=flat[width : 2 * width],
                heads=flat[2 * width :].reshape(2, HD),
            )
        )

    owners = lax.dynamic_index_in_dim(pair_owner, core, 0, keepdims=False)
    index = (ring_order[:, None] * own_rows + jnp.arange(own_rows, dtype=jnp.int32)).reshape(-1)
    inv_freq = ROPE_BASE ** (-jnp.arange(0, HD, 2).astype(F32) / HD)
    seq_tables = []
    for seq in range(SEQS):
        block = jnp.take(owners[seq], ctx ^ jnp.arange(n_ctx, dtype=jnp.int32))[:, None]
        k_pos = jnp.where(
            index < STRETCH,
            block * STRETCH + index,
            (2 * n_ctx - 1 - block) * STRETCH + index - STRETCH,
        )
        q_pos = k_pos[0][:, None]
        angles = q_pos.astype(F32) * inv_freq[None, :]
        cosine, sine = jnp.cos(angles), jnp.sin(angles)
        seq_tables.append(
            (
                jnp.concatenate([cosine, cosine, -sine, sine], axis=1),
                q_pos,
                k_pos,
            )
        )

    q_width, kv_width, ff = w_query.shape[2], w_key.shape[2], w_gate.shape[2]
    widths = {
        QKV: (q_width, kv_width, kv_width),
        OUT: (width,),
        GATE_UP: (ff, ff),
        DOWN: (width,),
    }
    qkv, output, gate, up, down = zip(own, other)
    weights = SimpleNamespace(qkv=qkv, output=output, gate=gate, up=up, down=down)
    driver = Driver(raw_own)
    driver.add(gather_lane(driver, RAW, raw_own, (), other), 0)
    for seq in range(SEQS):
        driver.add(
            sequence_lane(
                driver, seq, weights, gains, seq_tables[seq], own_rows, in_ring_order
            ),
            0,
            seq,
        )
    driver.add(gather_lane(driver, TOP, top_own, (RAW,)), 1)
    for layer in (1, 0):
        for name, cost in MATRICES:
            way = WAYS[layer][name]
            urgent = layer == 0
            lane = matrix_lane(driver, name, layer, cost, way)
            driver.add(lane, 1 if urgent else 3, (name, layer), URGENT if urgent else 3.0)
    for name, _ in MATRICES:
        driver.add(assemble_lane(driver, name, widths[name]), 2)
    driver.add(home_lane(driver, INPUT_GRAD), 1)
    driver.add(home_lane(driver, OUTPUT, ((HOME, INPUT_GRAD),)), 4)
    driver.add(gain_lane(driver), 2)
    driver.run()
    LOGS.append(driver.log)

    def made(key):
        return driver.store[key][1]

    flat = lax.dynamic_index_in_dim(made(GAINS), core, 0, keepdims=False)
    g_query, g_key, g_value = [x[None] for x in made((WHOLE, QKV))]
    g_gate, g_up = [x[None] for x in made((WHOLE, GATE_UP))]
    g_output, g_down = [made((WHOLE, x))[0][None] for x in (OUT, DOWN)]
    return (
        made((HOME, OUTPUT))[None],
        made((HOME, INPUT_GRAD))[None],
        flat[:width][None],
        g_query,
        g_key,
        g_value,
        flat[2 * width : 2 * width + HD][None],
        flat[2 * width + HD :][None],
        g_output,
        flat[width : 2 * width][None],
        g_gate,
        g_up,
        g_down,
    )


def solution(mesh):
    in_specs = (
        P(None, (CTX, MP), None),
        P(None, (CTX, MP), None),
        P(),
        P(CORES, None),
        P(CORES, None, MP),
        P(CORES, None, MP),
        P(CORES, None, MP),
        P(CORES, None),
        P(CORES, None),
        P(CORES, MP, None),
        P(CORES, None),
        P(CORES, None, MP),
        P(CORES, None, MP),
        P(CORES, MP, None),
    )
    out_specs = (
        P(CORES, None, (CTX, MP), None),
        P(CORES, None, (CTX, MP), None),
        P(CORES, None),
        P(CORES, None, MP),
        P(CORES, None, MP),
        P(CORES, None, MP),
        P(CORES, None),
        P(CORES, None),
        P(CORES, MP, None),
        P(CORES, None),
        P(CORES, None, MP),
        P(CORES, None, MP),
        P(CORES, MP, None),
    )
    return jax.shard_map(shards, mesh=mesh, in_specs=in_specs, out_specs=out_specs, check_vma=False)
```

```python
import functools
from types import SimpleNamespace

import jax
import jax.numpy as jnp
from jax import lax
from jax.experimental import pallas as pl
from jax.experimental.pallas import tpu as pltpu
from jax.sharding import PartitionSpec as P

HD = 128
LANES = 128
MB = 2
SEQS = 2
STRETCH = 128
EPSILON = 1e-06
ROPE_BASE = 1000000.0
MASKED_SCORE = -1e30
SCALING = HD ** (-0.5)
LOW = jnp.bfloat16
F32 = jnp.float32
VMEM_SPARE = 12 * 1024 * 1024
VMEM_LEAST = 50 * 1024 * 1024


def dot_nn(left, right):
    return lax.dot_general(left, right, (((1,), (0,)), ((), ())), preferred_element_type=F32)


def dot_nt(left, right):
    return lax.dot_general(left, right, (((1,), (1,)), ((), ())), preferred_element_type=F32)


def dot_tn(left, right):
    return lax.dot_general(left, right, (((0,), (0,)), ((), ())), preferred_element_type=F32)


def kernel_call(body, out_shape, flops, args, layer, weights):
    held = [jax.ShapeDtypeStruct(x.shape, x.dtype) for x in (*args, *[w[0] for w in weights])]
    moved = sum(x.size * x.dtype.itemsize for x in (*held, *out_shape))
    n_args, n_weights, n_out = len(args), len(weights), len(out_shape)

    def whole(*refs):
        ins, rest = refs[:n_args], refs[n_args:]
        pairs, rest = rest[: 2 * n_weights], rest[2 * n_weights :]
        outs, here, sems = rest[:n_out], rest[n_out:-1], rest[-1]
        home = lax.axis_index(CORES) == layer

        def copy(i, source):
            return pltpu.make_async_copy(source, here[i], sems.at[i])

        for i, ref in enumerate(ins):
            copy(i, ref).start()
        for which, taken in ((0, home), (1, jnp.logical_not(home))):

            @pl.when(taken)
            def _(which=which):
                for i in range(n_weights):
                    copy(n_args + i, pairs[2 * i + which]).start()

        def arrived(i):
            copy(n_args + i, pairs[2 * i]).wait()
            return here[n_args + i]

        for i, ref in enumerate(ins):
            copy(i, ref).wait()
        gets = [functools.partial(arrived, i) for i in range(n_weights)]
        body(*here[:n_args], *gets, *outs)

    vmem, hbm = pl.BlockSpec(memory_space=pltpu.VMEM), pl.BlockSpec(memory_space=pltpu.HBM)
    return pl.pallas_call(
        whole,
        out_shape=out_shape,
        in_specs=[hbm] * (n_args + 2 * n_weights),
        out_specs=[vmem] * n_out,
        scratch_shapes=[pltpu.VMEM(x.shape, x.dtype) for x in held]
        + [pltpu.SemaphoreType.DMA((len(held),))],
        compiler_params=pltpu.CompilerParams(vmem_limit_bytes=max(moved + VMEM_SPARE, VMEM_LEAST)),
        cost_estimate=pl.CostEstimate(flops=flops, bytes_accessed=moved, transcendentals=0),
    )(*args, *[ref for w in weights for ref in w])


def qkv_forward_body(q_width, x, gains, turns, get_qkv, proj, queries, kv):
    cos_full, sin_signed = turns[:, :HD], turns[:, HD:]

    def prepared(head, gain):
        scaling = lax.rsqrt(jnp.mean(head * head, axis=-1, keepdims=True) + EPSILON)
        normed = head * scaling * gain
        return (normed * cos_full + pltpu.roll(normed, HD // 2, 1) * sin_signed).astype(LOW)

    mixed = dot_nn(x[...], get_qkv()[...])
    both = proj.shape[1]
    proj[...] = mixed[:, :both]
    for at in range(0, q_width, HD):
        queries[:, at : at + HD] = prepared(mixed[:, at : at + HD], gains[:1, :])
    for at in range(q_width, both, HD):
        kv[:, at - q_width : at - q_width + HD] = prepared(mixed[:, at : at + HD], gains[1:, :])
    kv[:, both - q_width :] = mixed[:, both:].astype(LOW)


def mlp_forward_body(x, get_gate, get_up, get_down, gate, up, hidden, *parts):
    rows = x[...]
    gate_all = dot_nn(rows, get_gate()[...])
    up_all = dot_nn(rows, get_up()[...])
    gate[...] = gate_all.astype(LOW)
    up[...] = up_all.astype(LOW)
    hidden[...] = (jax.nn.silu(gate_all) * up_all).astype(LOW)
    store_product(parts, hidden[...], get_down(), dot_nn)


def mlp_back_body(branch, gate, up, get_down, get_gate, get_up, grad_gate, grad_up, *parts):
    grad_hidden = dot_nt(branch[...], get_down()[...])
    gate_all, up_all = gate[...].astype(F32), up[...].astype(F32)
    sig = jax.nn.sigmoid(gate_all)
    grad_gate[...] = (grad_hidden * up_all * sig * (1.0 + gate_all * (1.0 - sig))).astype(LOW)
    grad_up[...] = (grad_hidden * gate_all * sig).astype(LOW)
    w_gate, w_up = get_gate(), get_up()
    for at in range(0, w_gate.shape[0], 512):
        here = pl.ds(at, 512)
        total = dot_nt(grad_gate[...], w_gate[here, :]) + dot_nt(grad_up[...], w_up[here, :])
        store_columns(parts, here, total)


def store_columns(parts, here, rows):
    size = parts[0].shape[0]
    for i, part in enumerate(parts):
        part[:, here] = rows[i * size : (i + 1) * size].astype(LOW)


def store_product(parts, rows, weight, dot):
    for at in range(0, weight.shape[1], 512):
        here = pl.ds(at, 512)
        store_columns(parts, here, dot(rows, weight[:, here]))


def store_blocks(parts, rows):
    size = parts[0].shape[0]
    for i, part in enumerate(parts):
        part[...] = rows[i * size : (i + 1) * size].astype(LOW)


def attend_body(n_ctx, queries, *refs):
    blocks = refs[:n_ctx]
    q_pos, k_pos, get_out = refs[n_ctx : n_ctx + 3]
    attended, log_total, *parts = refs[n_ctx + 3 :]
    rows = queries.shape[0]
    kv_width = blocks[0].shape[1] // 2
    groups = queries.shape[1] // kv_width
    place = jnp.concatenate([q_pos[...]] * groups, axis=0)
    for kv_head in range(kv_width // HD):
        first = kv_head * groups
        stacked = jnp.concatenate(
            [queries[:, (first + i) * HD : (first + i + 1) * HD] for i in range(groups)], axis=0
        )
        at = kv_head * HD
        scores = []
        for j, block in enumerate(blocks):
            raw = dot_nt(stacked, block[:, at : at + HD]) * SCALING
            scores.append(jnp.where(k_pos[j : j + 1, :] <= place, raw, MASKED_SCORE))
        top = functools.reduce(
            jnp.maximum, [jnp.max(s, axis=1, keepdims=True) for s in scores]
        )
        total, running = 0.0, 0.0
        for s, block in zip(scores, blocks):
            weights = jnp.exp(s - top)
            total = total + jnp.sum(weights, axis=1, keepdims=True)
            running = running + dot_nn(
                weights.astype(LOW), block[:, kv_width + at : kv_width + at + HD]
            )
        result = (running / total).astype(LOW)
        logs = top + jnp.log(total)
        for i in range(groups):
            head = first + i
            attended[:, head * HD : (head + 1) * HD] = result[i * rows : (i + 1) * rows]
            log_total[:, head : head + 1] = logs[i * rows : (i + 1) * rows]
    store_blocks(parts, dot_nn(attended[...], get_out()[...]))


def attend_back_body(n_ctx, grad_rows, queries, *refs):
    blocks = refs[:n_ctx]
    q_pos, k_pos, attended, log_total, get_out, grad_q = refs[n_ctx : n_ctx + 6]
    grad_kv = refs[n_ctx + 6 :]
    rows = queries.shape[0]
    kv_width = blocks[0].shape[1] // 2
    groups = queries.shape[1] // kv_width
    grad_all = dot_nt(grad_rows[...], get_out()[...]).astype(LOW)
    place = jnp.concatenate([q_pos[...]] * groups, axis=0)
    for kv_head in range(kv_width // HD):
        heads = [kv_head * groups + i for i in range(groups)]
        stacked = jnp.concatenate([queries[:, h * HD : (h + 1) * HD] for h in heads], axis=0)
        grads = jnp.concatenate([grad_all[:, h * HD : (h + 1) * HD] for h in heads], axis=0)
        out_low = jnp.concatenate([attended[:, h * HD : (h + 1) * HD] for h in heads], axis=0)
        logs = jnp.concatenate([log_total[:, h : h + 1] for h in heads], axis=0)
        delta = jnp.sum(grads.astype(F32) * out_low.astype(F32), axis=1, keepdims=True)
        at = kv_head * HD
        total = 0.0
        for j, block in enumerate(blocks):
            keys = block[:, at : at + HD]
            values = block[:, kv_width + at : kv_width + at + HD]
            shifted = dot_nt(stacked, keys) * SCALING - logs
            probs = jnp.exp(jnp.where(k_pos[j : j + 1, :] <= place, shifted, MASKED_SCORE))
            grad_scores = (probs * (dot_nt(grads, values) - delta)).astype(LOW)
            total = total + dot_nn(grad_scores, keys)
            grad_kv[j][:, at : at + HD] = (dot_tn(grad_scores, stacked) * SCALING).astype(LOW)
            grad_kv[j][:, kv_width + at : kv_width + at + HD] = dot_tn(
                probs.astype(LOW), grads
            ).astype(LOW)
        for i, h in enumerate(heads):
            grad_q[:, h * HD : (h + 1) * HD] = total[i * rows : (i + 1) * rows] * SCALING


def qkv_back_body(n_ctx, grad_q, *refs):
    grad_kv = refs[:n_ctx]
    proj, gains, turns, get_qkv, mixed, grad_gains, *parts = refs[n_ctx:]
    cos_full, sin_signed = turns[:, :HD], turns[:, HD:]
    q_width = grad_q.shape[1]
    kv_width = proj.shape[1] - q_width

    def pulled(grad, head, gain):
        turned = grad * cos_full + pltpu.roll(grad * sin_signed, HD // 2, 1)
        scaling = lax.rsqrt(jnp.mean(head * head, axis=-1, keepdims=True) + EPSILON)
        inner = turned * gain
        back = scaling * inner - head * (
            scaling * scaling * scaling * jnp.mean(inner * head, axis=-1, keepdims=True)
        )
        return back.astype(LOW), jnp.sum(turned * head * scaling, axis=0, keepdims=True)

    total = 0.0
    for at in range(0, q_width, HD):
        back, gain_part = pulled(grad_q[:, at : at + HD], proj[:, at : at + HD], gains[:1, :])
        mixed[:, at : at + HD] = back
        total = total + gain_part
    grad_gains[:1, :] = total
    summed = functools.reduce(jnp.add, [g[...].astype(F32) for g in grad_kv])
    total = 0.0
    for at in range(0, kv_width, HD):
        here = slice(q_width + at, q_width + at + HD)
        back, gain_part = pulled(summed[:, at : at + HD], proj[:, here], gains[1:, :])
        mixed[:, here] = back
        total = total + gain_part
    grad_gains[1:, :] = total
    mixed[:, q_width + kv_width :] = summed[:, kv_width:].astype(LOW)
    w_qkv = get_qkv()
    for at in range(0, w_qkv.shape[0], 512):
        here = pl.ds(at, 512)
        store_columns(parts, here, dot_nt(mixed[...], w_qkv[here, :]))


def product_body(n_left, n_right, place, *refs):
    lefts, refs = refs[:n_left], refs[n_left:]
    groups = []
    for count in n_right:
        groups.append(refs[:count])
        refs = refs[count:]
    *extra, out, left_all, right_all, sems = refs
    tile, rows = out.shape[0], left_all.shape[1]
    step = pl.program_id(0)

    @pl.when(step == 0)
    def _():
        copies = []
        row = 0
        for ref in lefts:
            source = ref.at[:, pl.ds(pl.multiple_of(place[0] * rows, rows), rows)]
            copies.append((source, left_all.at[pl.ds(row, ref.shape[0]), :]))
            row += ref.shape[0]
        column = 0
        for group in groups:
            row = 0
            for ref in group:
                here = (pl.ds(row, ref.shape[0]), pl.ds(column, ref.shape[1]))
                copies.append((ref, right_all.at[here]))
                row += ref.shape[0]
            column += group[0].shape[1]
        copies = [
            pltpu.make_async_copy(source, target, sems.at[i])
            for i, (source, target) in enumerate(copies)
        ]
        for copy in copies:
            copy.start()
        for copy in copies:
            copy.wait()

    left = left_all[:, pl.ds(pl.multiple_of(step * tile, tile), tile)]
    width = 512
    for at in range(0, out.shape[1], width):
        result = dot_tn(left, right_all[:, at : at + width])
        if extra:
            result = result + extra[0][:, at : at + width].astype(F32)
        out[:, at : at + width] = result.astype(LOW)


def piece_product(pieces, which, lefts, rights, extra=None, extra_at=0):
    depth = sum(x.shape[0] for x in lefts)
    rows = lefts[0].shape[1] // pieces
    cols = sum(group[0].shape[1] for group in rights)
    tile = 256
    while rows % tile:
        tile //= 2
    steps = rows // tile
    flat = [x for group in rights for x in group]
    extras = [] if extra is None else [extra]
    place = jnp.stack([jnp.asarray(which, jnp.int32), jnp.asarray(extra_at, jnp.int32)])
    held = 2 * depth * (rows + cols)
    return pl.pallas_call(
        functools.partial(product_body, len(lefts), [len(group) for group in rights]),
        out_shape=jax.ShapeDtypeStruct((rows, cols), LOW),
        grid_spec=pltpu.PrefetchScalarGridSpec(
            num_scalar_prefetch=1,
            grid=(steps,),
            in_specs=[pl.BlockSpec(memory_space=pltpu.HBM)] * (len(lefts) + len(flat))
            + [
                pl.BlockSpec((tile, cols), lambda i, place: (place[1] * steps + i, 0))
                for _ in extras
            ],
            out_specs=pl.BlockSpec((tile, cols), lambda i, place: (i, 0)),
            scratch_shapes=[
                pltpu.VMEM((depth, rows), LOW),
                pltpu.VMEM((depth, cols), LOW),
                pltpu.SemaphoreType.DMA((len(lefts) + len(flat),)),
            ],
        ),
        compiler_params=pltpu.CompilerParams(
            vmem_limit_bytes=max(held + 8 * tile * cols + VMEM_SPARE, VMEM_LEAST)
        ),
        cost_estimate=pl.CostEstimate(
            flops=2 * depth * rows * cols,
            bytes_accessed=held + 2 * rows * cols * (1 + len(extras)),
            transcendentals=0,
        ),
    )(place, *lefts, *flat, *extras)


def assemble_body(widths, place, *refs):
    ins, outs = refs[:4], refs[4:]
    step = pl.program_id(0)
    for i in range(4):

        @pl.when((step == i % 2) & (place[0] == i // 2))
        def _(i=i):
            at = 0
            for out, width in zip(outs, widths):
                out[...] = ins[i][:, at : at + width].astype(F32)
                at += width


def assemble(place, arrays, widths):
    rows, cols = arrays[0].shape
    tile = 256
    while rows % tile:
        tile //= 2
    steps = rows // tile

    def in_map(i, step, t, place):
        wanted = place[0] == i // 2
        if i % 2 == 0:
            moving = jnp.where(step == 0, t, steps - 1)
        else:
            moving = jnp.where(step == 0, 0, t)
        return (jnp.where(wanted, moving, 0), 0)

    def out_map(step, t, place):
        return ((place[0] ^ step) * steps + t, 0)

    return pl.pallas_call(
        functools.partial(assemble_body, widths),
        out_shape=[jax.ShapeDtypeStruct((2 * rows, w), F32) for w in widths],
        grid_spec=pltpu.PrefetchScalarGridSpec(
            num_scalar_prefetch=1,
            grid=(2, steps),
            in_specs=[pl.BlockSpec((tile, cols), functools.partial(in_map, i)) for i in range(4)],
            out_specs=[pl.BlockSpec((tile, w), out_map) for w in widths],
        ),
        compiler_params=pltpu.CompilerParams(vmem_limit_bytes=24 * tile * cols + VMEM_SPARE),
        cost_estimate=pl.CostEstimate(
            flops=0, bytes_accessed=2 * rows * cols * 6, transcendentals=0
        ),
    )(place, *arrays)


Z_SLOT, Z_HOP = 5.5, 3.2


START_COST = 0.9
AHEAD = 10.0
RING, LINKS, SWAP, SPARSE, NONE = range(5)
RAW, TOP, OUTPUT, INPUT_GRAD, GAIN, GAINS, HALF, WHOLE, HOME, LATE, GATE_UP, DOWN, OUT, QKV = range(14)
CORES, CTX, MP = "section", "ctx", "mp"


class Send:
    def __init__(self, kind, blocks, span, then=0.0, slack=0.0):
        self.kind, self.blocks, self.span, self.then, self.slack = kind, blocks, span, then, slack


class Need:
    def __init__(self, *keys, then=0.0):
        self.keys, self.then = keys, then


class Wait:
    def __init__(self, until):
        self.until = until


class Lane:
    def __init__(self, work, rank, name, patience):
        self.work, self.rank, self.name, self.patience = work, rank, name, patience
        self.ready, self.value, self.wanted, self.then = 0.0, None, None, 0.0


class Driver:
    def __init__(self, token):
        self.token, self.now, self.cost = token, 0.0, 0.0
        self.lanes, self.store, self.log = [], {}, []
        self.free = [0.0] * 5

    def spend(self, cost):
        self.cost += cost

    def put(self, key, value):
        self.store[key] = (self.now + self.cost, value)

    def add(self, work, rank, name=None, patience=3.0):
        lane = Lane(work, rank, name, patience)
        lane.ready = self.now
        self.lanes.append(lane)

    def tied(self, value):
        leaves, tree = jax.tree.flatten(value)
        if not leaves:
            return value
        *leaves, _ = lax.optimization_barrier((*leaves, self.token))
        return jax.tree.unflatten(tree, leaves)

    def turn(self):
        while self.free[LINKS] > self.now + AHEAD:
            yield Wait(self.free[LINKS] - AHEAD)

    def ready_at(self, lane):
        if lane.wanted is None:
            return lane.ready
        if any(key not in self.store for key in lane.wanted):
            return None
        return max([lane.ready] + [self.store[key][0] for key in lane.wanted])

    def step(self, lane):
        self.log.append((self.now, self.ready_at(lane), lane.name))
        self.now = max(self.now, self.ready_at(lane))
        if lane.wanted is not None:
            lane.value = tuple(self.store[key][1] for key in lane.wanted)
            lane.wanted = None
        self.cost = 0.0
        value = None if lane.value is None else self.tied(lane.value)
        lane.value = None
        try:
            request = lane.work.send(value)
        except StopIteration:
            self.lanes.remove(lane)
            self.now += self.cost
            return
        self.now += self.cost
        if isinstance(request, Wait):
            lane.ready = max(self.now, request.until)
            return
        lane.then = request.then
        if isinstance(request, Need):
            lane.wanted, lane.ready = request.keys, self.now
            return
        self.now += START_COST * len(request.blocks)
        start = max(self.now, self.free[request.kind])
        self.free[request.kind] = start + request.span
        lane.ready = start + request.span + Z_HOP + request.slack
        lane.value = [move(block) for move, block in request.blocks]
        self.token = request.blocks[0][1]

    def run(self):
        while self.lanes:
            times = [(self.ready_at(lane), lane) for lane in self.lanes]
            times = [(at, lane) for at, lane in times if at is not None]
            main = [pair for pair in times if pair[1].rank == 0]
            soon = min([at for at, _ in main], default=1e9)
            waiting = [
                (at, lane)
                for at, lane in times
                if at <= self.now
                and (lane.rank == 0 or max(self.now, at) + lane.then <= soon + lane.patience)
            ]
            if waiting:
                lane = min(waiting, key=lambda pair: (pair[1].rank, pair[0]))[1]
            elif main:
                lane = min(
                    [p for p in times if p[1].rank == 0 or p[0] + p[1].then <= soon + p[1].patience],
                    key=lambda pair: (pair[0], pair[1].rank),
                )[1]
            else:
                lane = min(times, key=lambda pair: (pair[0], pair[1].rank))[1]
            self.step(lane)


def swap_cores(block):
    return lax.ppermute(block, CORES, [(0, 1), (1, 0)])


def to_core(core):
    return lambda block: lax.ppermute(block, CORES, [(1 - core, core)])


def ring_step(block):
    count = lax.axis_size(MP)
    return lax.ppermute(block, MP, [(i, (i + 1) % count) for i in range(count)])


def across_ctx(distance):
    count = lax.axis_size(CTX)
    return lambda block: lax.ppermute(block, CTX, [(i, i ^ distance) for i in range(count)])


def ring_gather(driver, block):
    blocks = [block]
    for _ in range(lax.axis_size(MP) - 1):
        (block,) = yield Send(RING, [(ring_step, block)], Z_SLOT)
        blocks.append(block)
    driver.spend(1.5)
    return lax.optimization_barrier(jnp.concatenate(blocks, axis=0))


def ring_sum(driver, part):
    count = lax.axis_size(MP)
    if not isinstance(part, list):
        rows = part.shape[0] // count
        part = [part[t * rows : (t + 1) * rows] for t in range(count)]
        driver.spend(0.8)
    running = part[1]
    for t in range(2, count):
        (got,) = yield Send(RING, [(ring_step, running)], Z_SLOT)
        running = (got.astype(F32) + part[t].astype(F32)).astype(LOW)
        driver.spend(1.4)
    (got,) = yield Send(RING, [(ring_step, running)], Z_SLOT)
    driver.spend(1.4)
    return got.astype(F32) + part[0].astype(F32)


def ctx_exchange(blocks, span=12.0):
    moves = [(across_ctx(j + 1), block) for j, block in enumerate(blocks)]
    got = yield Send(LINKS, moves, span)
    return got


def summed_everywhere(driver, block):
    for axis in (MP, CORES, CTX):
        count = lax.axis_size(axis)
        distance = 1
        while distance < count:
            route = [(i, i ^ distance) for i in range(count)]
            (got,) = yield Send(
                LINKS if axis == CTX else NONE,
                [(functools.partial(lax.ppermute, axis_name=axis, perm=route), block)],
                2.0,
                1.0,
                5.0,
            )
            block = block + got
            driver.spend(1.0)
            distance *= 2
    return block


def row_norm(rows, gain):
    scaling = lax.rsqrt(jnp.mean(rows * rows, axis=-1, keepdims=True) + EPSILON)
    return rows * scaling * gain


def row_norm_back(rows, gain, grad):
    scaling = lax.rsqrt(jnp.mean(rows * rows, axis=-1, keepdims=True) + EPSILON)
    inner = grad * gain
    back = scaling * inner - rows * (
        scaling * scaling * scaling * jnp.mean(inner * rows, axis=-1, keepdims=True)
    )
    return back, jnp.sum(grad * rows * scaling, axis=0)


def shape(rows, cols, kind=LOW):
    return jax.ShapeDtypeStruct((rows, cols), kind)


def part_shapes(rows, width):
    count = lax.axis_size(MP)
    return [shape(rows // count, width)] * count


def project(attn_in, layer, weights, gains, tables):
    turns, q_pos, k_pos = tables
    rows, width = attn_in.shape
    total = weights.qkv[0].shape[1]
    q_width = weights.output[0].shape[0]
    kv_width = (total - q_width) // 2
    return kernel_call(
        functools.partial(qkv_forward_body, q_width),
        [shape(rows, q_width + kv_width, F32), shape(rows, q_width), shape(rows, 2 * kv_width)],
        2 * rows * width * total,
        (attn_in, gains.heads, turns),
        layer,
        [weights.qkv],
    )


def attend(queries, blocks, layer, weights, tables):
    turns, q_pos, k_pos = tables
    rows, q_width = queries.shape
    width = weights.output[0].shape[1]
    attended, log_total, *parts = kernel_call(
        functools.partial(attend_body, len(blocks)),
        [shape(rows, q_width), shape(rows, q_width // HD, F32)] + part_shapes(rows, width),
        2 * rows * q_width * (2 * rows * len(blocks) + width),
        (queries, *blocks, q_pos, k_pos),
        layer,
        [weights.output],
    )
    return parts, attended, log_total


def mlp_forward(mlp_in, layer, weights):
    ff = weights.gate[0].shape[1]
    picked = [weights.gate, weights.up, weights.down]
    rows, width = mlp_in.shape
    gate, up, hidden, *parts = kernel_call(
        mlp_forward_body,
        [shape(rows, ff)] * 3 + part_shapes(rows, width),
        6 * rows * width * ff,
        (mlp_in,),
        layer,
        picked,
    )
    return gate, up, hidden, parts


def mlp_back(branch, kept, layer, weights):
    ff = weights.gate[0].shape[1]
    picked = [weights.down, weights.gate, weights.up]
    rows, width = branch.shape
    grad_gate, grad_up, *parts = kernel_call(
        mlp_back_body,
        [shape(rows, ff)] * 2 + part_shapes(rows, width),
        6 * rows * width * ff,
        (branch, kept.gate, kept.up),
        layer,
        picked,
    )
    return grad_gate, grad_up, parts


def attend_back(grad_rows, kept, layer, weights, tables):
    turns, q_pos, k_pos = tables
    blocks = kept.blocks
    rows, q_width = kept.queries.shape
    return kernel_call(
        functools.partial(attend_back_body, len(blocks)),
        [shape(rows, q_width, F32)] + [shape(*blocks[0].shape)] * len(blocks),
        2 * rows * q_width * (5 * rows * len(blocks) + grad_rows.shape[1]),
        (
            grad_rows,
            kept.queries,
            *blocks,
            q_pos,
            k_pos,
            kept.attended,
            kept.log_total,
        ),
        layer,
        [weights.output],
    )


def project_back(grad_q, grad_kv, kept, layer, weights, gains, tables):
    turns, q_pos, k_pos = tables
    rows, width = kept.attn_in.shape
    total = weights.qkv[0].shape[1]
    mixed, grad_gains, *parts = kernel_call(
        functools.partial(qkv_back_body, len(grad_kv)),
        [shape(rows, total), shape(2, HD, F32)] + part_shapes(rows, width),
        2 * rows * width * total,
        (grad_q, *grad_kv, kept.proj, gains.heads, turns),
        layer,
        [weights.qkv],
    )
    return mixed, parts, grad_gains


def sequence_lane(driver, seq, weights, gains, tables, own_rows, in_ring_order):
    (raw,) = yield Need(RAW)
    rows = in_ring_order(raw, seq)
    h_rows = rows[:own_rows].astype(F32)
    kept = []
    for layer in range(2):
        gain = gains[layer]
        if layer == 0:
            attn_in = row_norm(rows.astype(F32), gain.attn).astype(LOW)
            driver.spend(4.0)
        else:
            attn_in = yield from ring_gather(driver, row_norm(h_rows, gain.attn).astype(LOW))
        proj, queries, kv = project(attn_in, layer, weights, gain, tables)
        driver.spend(6.0)
        others = yield from ctx_exchange([kv] * (lax.axis_size(CTX) - 1))
        blocks = [kv] + others
        part, attended, log_total = attend(queries, blocks, layer, weights, tables)
        driver.spend(6.0)
        mid = h_rows + (yield from ring_sum(driver, part))
        driver.spend(1.0)
        mlp_in = yield from ring_gather(driver, row_norm(mid, gain.mlp).astype(LOW))
        gate, up, hidden, part = mlp_forward(mlp_in, layer, weights)
        driver.spend(9.5)
        kept.append(
            SimpleNamespace(
                attn_in=attn_in,
                h_rows=h_rows,
                proj=proj,
                queries=queries,
                blocks=blocks,
                attended=attended,
                log_total=log_total,
                mid=mid,
                mlp_in=mlp_in,
                gate=gate,
                up=up,
                hidden=hidden,
            )
        )
        h_rows = mid + (yield from ring_sum(driver, part))
        driver.spend(1.0)
        driver.put((OUTPUT, layer, seq), h_rows)

    (top_grad,) = yield Need(TOP)
    branch = in_ring_order(top_grad, seq)
    driver.spend(2.0)
    grad_out = branch[:own_rows].astype(F32)
    for layer in (1, 0):
        gain, state = gains[layer], kept[layer]
        if layer == 0:
            branch = yield from ring_gather(driver, grad_out.astype(LOW))
        driver.put((DOWN, layer, seq), (state.hidden, branch))
        grad_gate, grad_up, part = mlp_back(branch, state, layer, weights)
        driver.spend(12.0)
        driver.put((GATE_UP, layer, seq), (state.mlp_in, grad_gate, grad_up))
        back, mlp_gain = row_norm_back(
            state.mid, gain.mlp, (yield from ring_sum(driver, part))
        )
        driver.spend(4.0)
        grad_mid = grad_out + back
        grad_rows = yield from ring_gather(driver, grad_mid.astype(LOW))
        driver.put((OUT, layer, seq), (state.attended, grad_rows))
        grad_q, *grad_kv = attend_back(grad_rows, state, layer, weights, tables)
        driver.spend(10.0)
        grad_kv = [grad_kv[0]] + (yield from ctx_exchange(grad_kv[1:], 17.0))
        mixed, part, head_gains = project_back(
            grad_q, grad_kv, state, layer, weights, gain, tables
        )
        driver.spend(9.0)
        driver.put((QKV, layer, seq), (state.attn_in, mixed))
        back, attn_gain = row_norm_back(
            state.h_rows, gain.attn, (yield from ring_sum(driver, part))
        )
        driver.spend(4.0)
        grad_out = grad_mid + back
        driver.put((INPUT_GRAD, layer, seq), grad_out)
        driver.put(
            (GAIN, layer, seq), jnp.concatenate([attn_gain, mlp_gain, head_gains.reshape(-1)])
        )


def core_bit(t, bits):
    shift = jnp.where(lax.axis_index(CORES) == 0, t, bits - 1 - t)
    return (lax.axis_index(CTX) >> shift) & 1


def joint_step(t, bits):
    count = 1 << bits
    route = []
    for core in range(2):
        distance = 1 << (t if core == 0 else bits - 1 - t)
        route += [(core * count + i, core * count + (i ^ distance)) for i in range(count)]
    return lambda block: lax.ppermute(block, (CORES, CTX), route)


def sum_by_halving(driver, product, rows, cost, slack):
    core = lax.axis_index(CORES)
    bits = lax.axis_size(CTX).bit_length() - 1
    flag = core_bit(0, bits)
    sent = None
    if rows % (4 * LANES) == 0:
        sent = product(4, 2 * core + 1 - flag, 1 - flag)
        total = product(4, 2 * core + flag, flag)
    else:
        total = product(2, core, 0)
    driver.spend(cost * 1.4)
    for t in range(bits):
        if sent is None:
            flag, count = core_bit(t, bits), total.shape[0] // 2
            sent = lax.dynamic_slice_in_dim(total, (1 - flag) * count, count, axis=0)
            total = lax.dynamic_slice_in_dim(total, flag * count, count, axis=0)
            driver.spend(1.5 + sent.size * 2 / 1e6)
        size = sent.size * 2 / 1e6
        (got,) = yield Send(
            LINKS, [(joint_step(t, bits), sent)], 11.5 * size, 1.5 + size, slack + 6.0 * size
        )
        driver.spend(1.0 + size)
        total = (total.astype(F32) + got.astype(F32)).astype(LOW)
        sent = None
    for t in reversed(range(bits)):
        size = total.size * 2 / 1e6
        (got,) = yield Send(
            LINKS, [(joint_step(t, bits), total)], 11.5 * size, 1.5 + 2 * size, slack + 6.0 * size
        )
        flag = core_bit(t, bits) == 0
        total = jnp.concatenate(
            [jnp.where(flag, total, got), jnp.where(flag, got, total)], axis=0
        )
        driver.spend(1.5 + 2 * size)
    return total


def scattered(driver, product, cost, crowding):
    total = product(2, lax.axis_index(CORES), 0)
    driver.spend(cost * 1.2)
    move = functools.partial(lax.psum_scatter, axis_name=CTX, scatter_dimension=0, tiled=True)
    span = (13 + 2e-5 * total.size) * crowding
    (share,) = yield Send(SPARSE, [(move, total)], span, 1.0)
    return share, span


def sum_by_collectives(driver, product, rows, cost, slack):
    share, span = yield from scattered(driver, product, cost, 1.0)
    move = functools.partial(lax.all_gather, axis_name=CTX, axis=0, tiled=True)
    (total,) = yield Send(SPARSE, [(move, share)], span, 1.0)
    return total


def sum_by_both(driver, product, rows, cost, slack):
    if lax.axis_size(CTX) != 4:
        return (yield from sum_by_collectives(driver, product, rows, cost, slack))
    share, _ = yield from scattered(driver, product, cost, 1.35)
    first = lax.axis_index(CORES) == 0
    size = share.size * 2 / 1e6
    (got,) = yield Send(
        LINKS, [(joint_step(0, 2), share)], 11.5 * size, 1.5 + 2 * size, slack + 3.0 * size
    )
    flag = core_bit(0, 2) == 0
    pair = jnp.stack([jnp.where(flag, share, got), jnp.where(flag, got, share)])
    driver.spend(1.5 + 2 * size)
    driver.put((LATE, share.shape[1]), ())
    (got,) = yield Send(
        LINKS, [(joint_step(1, 2), pair)], 23.0 * size, 2.0 + 4 * size, slack + 6.0 * size
    )
    flag = core_bit(1, 2) == 0
    low, high = jnp.where(flag, pair, got), jnp.where(flag, got, pair)
    driver.spend(2.0 + 4 * size)
    return jnp.concatenate(
        [
            low[0],
            jnp.where(first, low[1], high[0]),
            jnp.where(first, high[0], low[1]),
            high[1],
        ],
        axis=0,
    )


def matrix_lane(driver, name, layer, cost, way):
    parts = yield Need(*[(name, layer, seq) for seq in range(SEQS)], then=cost)
    lefts = [part[0] for part in parts]
    rights = [[part[at] for part in parts] for at in range(1, len(parts[0]))]
    driver.spend(cost)
    away = piece_product(2, 1 - lax.axis_index(CORES), lefts, rights)
    size = away.size * 2 / 1e6
    (received,) = yield Send(SWAP, [(swap_cores, away)], 2.0 + 1.6 * size, cost * 1.3, 4.0)

    def product(pieces, which, extra_at):
        return piece_product(pieces, which, lefts, rights, received, extra_at)

    slack = 4.0 if layer == 0 else 25.0
    half = yield from way(driver, product, lefts[0].shape[1], cost, slack)
    (other,) = yield Send(SWAP, [(to_core(layer), half)], 2.0 + 1.6 * size, 0.0, 4.0)
    driver.token = other
    driver.put((HALF, name, layer), (half, other))


def assemble_lane(driver, name, widths, after):
    if after:
        yield Need(after)
    first, second = yield Need((HALF, name, 0), (HALF, name, 1))
    core = lax.axis_index(CORES).astype(jnp.int32).reshape(1)
    whole = assemble(core, [*first, *second], widths)
    driver.token = whole[0]
    driver.put((WHOLE, name), whole)
    driver.spend(1.5 + 1.3e-6 * first[0].size * 4)


def home_lane(driver, name, after=()):
    if after:
        yield Need(*after)
    pairs = yield Need(*[(name, layer, seq) for seq in range(SEQS) for layer in range(2)])
    pairs = [pairs[2 * seq : 2 * seq + 2] for seq in range(SEQS)]
    core, place = lax.axis_index(CORES), lax.axis_index(MP)
    count = lax.axis_size(MP)
    even, half = place % 2 == 0, count // 2
    first_route = [(m, m // 2 if m % 2 == 0 else half + m // 2) for m in range(count)]
    second_route = [(m, half + m // 2 if m % 2 == 0 else m // 2) for m in range(count)]

    def within(route):
        return lambda block: lax.ppermute(block, MP, route)

    def across(route):
        pairs = [(k * count + a, (1 - k) * count + b) for k in range(2) for a, b in route]
        return lambda block: lax.ppermute(block, (CORES, MP), pairs)

    keep = [jnp.where(core == 0, a, b).astype(LOW) for a, b in pairs]
    send = [jnp.where(core == 0, b, a).astype(LOW) for a, b in pairs]
    moves = []
    for kind, rows in ((within, keep), (across, send)):
        moves.append((kind(first_route), jnp.where(even, rows[0], rows[1])))
        moves.append((kind(second_route), jnp.where(even, rows[1], rows[0])))
    driver.spend(4.0)
    got = yield Send(RING, moves, 4 * Z_SLOT, 2.0, 4.0)
    driver.token = got[-1]
    lower = place < half
    kept, other = [
        jnp.concatenate([jnp.where(lower, one, two), jnp.where(lower, two, one)], axis=0)
        for one, two in (got[:2], got[2:])
    ]
    whole = jnp.stack([jnp.where(core == 0, kept, other), jnp.where(core == 0, other, kept)])
    driver.put((HOME, name), whole.astype(F32))
    driver.spend(4.0)


def gain_lane(driver):
    got = yield Need(*[(GAIN, layer, seq) for layer in range(2) for seq in range(SEQS)])
    sums = jnp.stack([got[2 * layer] + got[2 * layer + 1] for layer in range(2)])
    driver.spend(2.0)
    driver.put(GAINS, (yield from summed_everywhere(driver, sums)))


def gather_lane(driver, name, block, after, beside=()):
    if after:
        yield Need(*after)
    (whole,) = yield Send(
        SPARSE, [(lambda x: lax.all_gather(x, MP, axis=0, tiled=True), block)], 46.0
    )
    if beside:
        whole, *_ = lax.optimization_barrier((whole, *beside))
    driver.token = whole
    driver.put(name, whole)


LOGS = []
MATRICES = ((GATE_UP, 9.5), (DOWN, 5.5), (OUT, 3.5), (QKV, 5.0))
WAYS = (
    {GATE_UP: sum_by_both, DOWN: sum_by_both, OUT: sum_by_halving, QKV: sum_by_halving},
    {
        GATE_UP: sum_by_collectives,
        DOWN: sum_by_collectives,
        OUT: sum_by_halving,
        QKV: sum_by_halving,
    },
)
URGENT = 12.0


def shards(
    section_input,
    cotangent,
    pair_owner,
    attn_gain,
    w_query,
    w_key,
    w_value,
    query_gain,
    key_gain,
    w_output,
    mlp_gain,
    w_gate,
    w_up,
    w_down,
):
    n_ctx, n_mp = lax.axis_size(CTX), lax.axis_size(MP)
    core, ctx, place = lax.axis_index(CORES), lax.axis_index(CTX), lax.axis_index(MP)
    is_first = core == 0
    width = section_input.shape[2]
    seq_rows = section_input.shape[1] * n_mp // SEQS
    own_rows = seq_rows // n_mp

    raw_own = lax.dynamic_index_in_dim(section_input, core, 0, keepdims=False)
    top_own = lax.dynamic_index_in_dim(cotangent, core, 0, keepdims=False).astype(LOW)
    ring_order = (place - jnp.arange(n_mp, dtype=jnp.int32)) % n_mp

    def in_ring_order(rows, seq):
        return jnp.concatenate(
            [
                lax.dynamic_slice_in_dim(
                    rows, seq * seq_rows + ring_order[t] * own_rows, own_rows, axis=0
                )
                for t in range(n_mp)
            ],
            axis=0,
        )

    w_qkv = jnp.concatenate([w_query[0], w_key[0], w_value[0]], axis=1)
    own = [w_qkv] + [w[0] for w in (w_output, w_gate, w_up, w_down)]
    other = [swap_cores(w) for w in own]
    own_gains = jnp.concatenate([attn_gain[0], mlp_gain[0], query_gain[0], key_gain[0]])
    other_gains = swap_cores(own_gains)
    gains = []
    for layer in range(2):
        mine = is_first if layer == 0 else ~is_first
        flat = jnp.where(mine, own_gains, other_gains).astype(F32)
        gains.append(
            SimpleNamespace(
                attn=flat[:width],
                mlp=flat[width : 2 * width],
                heads=flat[2 * width :].reshape(2, HD),
            )
        )

    owners = lax.dynamic_index_in_dim(pair_owner, core, 0, keepdims=False)
    index = (ring_order[:, None] * own_rows + jnp.arange(own_rows, dtype=jnp.int32)).reshape(-1)
    inv_freq = ROPE_BASE ** (-jnp.arange(0, HD, 2).astype(F32) / HD)
    seq_tables = []
    for seq in range(SEQS):
        block = jnp.take(owners[seq], ctx ^ jnp.arange(n_ctx, dtype=jnp.int32))[:, None]
        k_pos = jnp.where(
            index < STRETCH,
            block * STRETCH + index,
            (2 * n_ctx - 1 - block) * STRETCH + index - STRETCH,
        )
        q_pos = k_pos[0][:, None]
        angles = q_pos.astype(F32) * inv_freq[None, :]
        cosine, sine = jnp.cos(angles), jnp.sin(angles)
        seq_tables.append(
            (
                jnp.concatenate([cosine, cosine, -sine, sine], axis=1),
                q_pos,
                k_pos,
            )
        )

    q_width, kv_width, ff = w_query.shape[2], w_key.shape[2], w_gate.shape[2]
    widths = {
        QKV: (q_width, kv_width, kv_width),
        OUT: (width,),
        GATE_UP: (ff, ff),
        DOWN: (width,),
    }
    qkv, output, gate, up, down = zip(own, other)
    weights = SimpleNamespace(qkv=qkv, output=output, gate=gate, up=up, down=down)
    driver = Driver(raw_own)
    driver.add(gather_lane(driver, RAW, raw_own, (), other), 0)
    for seq in range(SEQS):
        driver.add(
            sequence_lane(
                driver, seq, weights, gains, seq_tables[seq], own_rows, in_ring_order
            ),
            0,
            seq,
        )
    driver.add(gather_lane(driver, TOP, top_own, (RAW,)), 1)
    for layer in (1, 0):
        for name, cost in MATRICES:
            way = WAYS[layer][name]
            urgent = layer == 0
            lane = matrix_lane(driver, name, layer, cost, way)
            driver.add(lane, 1 if urgent else 3, (name, layer), URGENT if urgent else 3.0)
    for name, _ in MATRICES:
        after = (LATE, 2 * ff) if name == DOWN and n_ctx == 4 else None
        driver.add(assemble_lane(driver, name, widths[name], after), 2)
    driver.add(home_lane(driver, INPUT_GRAD), 1)
    driver.add(home_lane(driver, OUTPUT, ((HOME, INPUT_GRAD),)), 4)
    driver.add(gain_lane(driver), 2)
    driver.run()
    LOGS.append(driver.log)

    def made(key):
        return driver.store[key][1]

    flat = lax.dynamic_index_in_dim(made(GAINS), core, 0, keepdims=False)
    g_query, g_key, g_value = [x[None] for x in made((WHOLE, QKV))]
    g_gate, g_up = [x[None] for x in made((WHOLE, GATE_UP))]
    g_output, g_down = [made((WHOLE, x))[0][None] for x in (OUT, DOWN)]
    return (
        made((HOME, OUTPUT))[None],
        made((HOME, INPUT_GRAD))[None],
        flat[:width][None],
        g_query,
        g_key,
        g_value,
        flat[2 * width : 2 * width + HD][None],
        flat[2 * width + HD :][None],
        g_output,
        flat[width : 2 * width][None],
        g_gate,
        g_up,
        g_down,
    )


def solution(mesh):
    in_specs = (
        P(None, (CTX, MP), None),
        P(None, (CTX, MP), None),
        P(),
        P(CORES, None),
        P(CORES, None, MP),
        P(CORES, None, MP),
        P(CORES, None, MP),
        P(CORES, None),
        P(CORES, None),
        P(CORES, MP, None),
        P(CORES, None),
        P(CORES, None, MP),
        P(CORES, None, MP),
        P(CORES, MP, None),
    )
    out_specs = (
        P(CORES, None, (CTX, MP), None),
        P(CORES, None, (CTX, MP), None),
        P(CORES, None),
        P(CORES, None, MP),
        P(CORES, None, MP),
        P(CORES, None, MP),
        P(CORES, None),
        P(CORES, None),
        P(CORES, MP, None),
        P(CORES, None),
        P(CORES, None, MP),
        P(CORES, None, MP),
        P(CORES, MP, None),
    )
    return jax.shard_map(shards, mesh=mesh, in_specs=in_specs, out_specs=out_specs, check_vma=False)
```
